32 devices in a mesh: dp: 4 (over x, core), seq: 8 (over z, y).
Axes of the slice: x: 2, y: 2, z: 4, core: 2. Of those that a mesh axis runs over, the one named last changes fastest.
Arguments:
- byte_ids: int32 [16, 4096], P('dp', 'seq'), may hold values from 0 to 255
- item_lengths: int32 [16], P('dp'), may hold values from 2048 to 4096, as said below
- block_counts: int32 [16], P('dp'), may hold values from 32 to 64, as said below
- byte_embed: bfloat16 [256, 512], replicated, may hold values from -6 to 6
- norm1_gain: float32 [512], replicated, may hold values from 0.25 to 1.75
- norm1_shift: float32 [512], replicated, may hold values from -4 to 4
- qkv_weight: bfloat16 [512, 1536], replicated, may hold values from -0.25 to 0.25
- out_weight: bfloat16 [512, 512], replicated, may hold values from -0.75 to 0.75
- norm2_gain: float32 [512], replicated, may hold values from 0.25 to 1.75
- norm2_shift: float32 [512], replicated, may hold values from -4 to 4
- up_weight: bfloat16 [512, 2048], replicated, may hold values from -0.25 to 0.25
- up_bias: float32 [2048], replicated, may hold values from -6 to 6
- down_weight: bfloat16 [2048, 512], replicated, may hold values from -0.125 to 0.125
- down_bias: float32 [512], replicated, may hold values from -4 to 4
- frontier_weight: float32 [512], replicated, may hold values from -0.25 to 0.25
- pooled_cot: float32 [16, 64, 512], P('dp'), may hold values from -6 to 6
Outputs:
- pooled: float32 [16, 64, 512], P('dp')
- embed_grad: float32 [256, 512], replicated
- norm1_gain_grad: float32 [512], replicated
- norm1_shift_grad: float32 [512], replicated
- qkv_grad: float32 [512, 1536], replicated
- out_grad: float32 [512, 512], replicated
- norm2_gain_grad: float32 [512], replicated
- norm2_shift_grad: float32 [512], replicated
- up_grad: float32 [512, 2048], replicated
- up_bias_grad: float32 [2048], replicated
- down_grad: float32 [2048, 512], replicated
- down_bias_grad: float32 [512], replicated
- frontier_grad: float32 [512], replicated
The draws below stay inside these ranges and needn't reach their ends.
Inputs may be any that keep to these rules, and one draw needn't show every extreme that they name: `item_lengths`: slots at or after an item's length are padding. Among the 4 items of each index of dp, one fills all 4096 slots. `block_counts`: some item has 64 blocks.
All inputs are finite; a program needn't handle non-finite values.
Results may differ from the reference program's by a relative error of at most 0.012.
The reference program's roundings to bfloat16 on the way count: a program that leaves them out, or rounds other values in their place, can miss the bound.
Values may be sent and summed in bfloat16 or wider, within the bound.
No kernel may reach another device: no remote copies, remote signals or barrier semaphores. Data moves between devices by JAX's collectives and lax.ppermute only.
A program may use at most 192 MiB of HBM per device.

```python
import jax
import jax.numpy as jnp
from jax import lax

D = 512
H = 8
HD = 64
FF = 2048
VOCAB = 256
WIN = 64
NB = 64
C = 512
ROWS_DEV = 4
ITEMS = 16
SEQ_LEN = 4096


def draw_item_lengths(key, part):
    key = jax.random.fold_in(key, 11)
    first_key, second_key = jax.random.split(key)
    lengths = jax.random.randint(first_key, (ITEMS,), SEQ_LEN // 2, SEQ_LEN + 1)
    chosen = jax.random.randint(second_key, (ITEMS // ROWS_DEV,), 0, ROWS_DEV)
    slots = jnp.arange(ITEMS) % ROWS_DEV
    groups = jnp.arange(ITEMS) // ROWS_DEV
    return jnp.where(slots == chosen[groups], SEQ_LEN, lengths).astype(jnp.int32)


def draw_block_counts(key, part):
    key = jax.random.fold_in(key, 23)
    first_key, second_key = jax.random.split(key)
    counts = jax.random.randint(first_key, (ITEMS,), NB // 2, NB + 1)
    chosen = jax.random.randint(second_key, (), 0, ITEMS)
    return jnp.where(jnp.arange(ITEMS) == chosen, NB, counts).astype(jnp.int32)


def with_ends(drawn, key, low, largest):
    index_at = [jax.random.randint(jax.random.fold_in(key, axis), (), 0, length) for axis, length in enumerate(drawn.shape)]
    main_axis = drawn.shape.index(max(drawn.shape))
    neighbour = index_at[:main_axis] + [(index_at[main_axis] + 1) % drawn.shape[main_axis]] + index_at[main_axis + 1:]
    return drawn.at[tuple(index_at)].set(low).at[tuple(neighbour)].set(largest)


def steps_of(own_key, dims, cuts, low, largest):
    loudness = 1.0
    for axis_at, parts in cuts:
        draws = jax.random.uniform(jax.random.fold_in(jax.random.fold_in(own_key, 6), axis_at), (parts,), jnp.float32, low / len(cuts), largest / len(cuts))
        loudness = loudness * jnp.repeat(jnp.exp(draws), dims[axis_at] // parts).reshape((-1,) + (1,) * (len(dims) - 1 - axis_at))
    return loudness


def scatter_about(stream_key, extent, scale, limit, pieces=(), held_as=jnp.bfloat16):
    array = jax.random.normal(stream_key, extent, jnp.float32) * scale
    if len(pieces) > 0:
        array = steps_of(stream_key, extent, pieces, -0.22, 0.18) * array
    return jnp.clip(array, min=-limit, max=limit).astype(held_as)


def setup_inputs(seed: int = 0) -> dict:
    arg_keys = jax.random.split(jax.random.key(seed), 17)
    byte_ids = with_ends(jax.random.randint(arg_keys[0], (ITEMS, SEQ_LEN), 0, VOCAB), jax.random.fold_in(arg_keys[0], 1), 0, VOCAB - 1).astype(jnp.int32)
    item_lengths = draw_item_lengths(jax.random.fold_in(arg_keys[16], 71), 0)
    block_counts = draw_block_counts(jax.random.fold_in(arg_keys[16], 71), 0)
    byte_embed = scatter_about(arg_keys[3], (VOCAB, D), 1.0, 6.0)
    norm1_gain = jnp.clip(1.0 + 0.15 * jax.random.normal(arg_keys[4], (D,), jnp.float32), 0.25, 1.75)
    norm1_shift = scatter_about(arg_keys[5], (D,), 0.3, 4.0, (), jnp.float32)
    qkv_weight = scatter_about(arg_keys[6], (D, 3 * D), D ** -0.5, 0.25)
    out_weight = scatter_about(arg_keys[7], (D, D), (D // 8) ** -0.5, 0.75)
    norm2_gain = jnp.clip(1.0 + 0.15 * jax.random.normal(arg_keys[8], (D,), jnp.float32), 0.25, 1.75)
    norm2_shift = scatter_about(arg_keys[9], (D,), 0.3, 4.0, (), jnp.float32)
    up_weight = scatter_about(arg_keys[10], (D, FF), D ** -0.5, 0.25)
    up_bias = scatter_about(arg_keys[11], (FF,), 0.5, 6.0, (), jnp.float32)
    down_weight = scatter_about(arg_keys[12], (FF, D), FF ** -0.5, 0.125)
    down_bias = scatter_about(arg_keys[13], (D,), 0.3, 4.0, (), jnp.float32)
    frontier_weight = scatter_about(arg_keys[14], (D,), D ** -0.5, 0.25, (), jnp.float32)
    pooled_cot = scatter_about(arg_keys[15], (ITEMS, NB, D), 1.0, 6.0, ((0, 4),), jnp.float32)
    return dict(byte_ids=byte_ids, item_lengths=item_lengths, block_counts=block_counts, byte_embed=byte_embed, norm1_gain=norm1_gain, norm1_shift=norm1_shift, qkv_weight=qkv_weight, out_weight=out_weight, norm2_gain=norm2_gain, norm2_shift=norm2_shift, up_weight=up_weight, up_bias=up_bias, down_weight=down_weight, down_bias=down_bias, frontier_weight=frontier_weight, pooled_cot=pooled_cot)


@jax.custom_vjp
def low(v):
    return lax.optimization_barrier(v.astype(jnp.bfloat16)).astype(jnp.float32)

@jax.custom_vjp
def low_back(v):
    return v

def low_keep(v):
    return (low(v), None)

def low_pass(kept, grad):
    return (grad,)

def back_keep(v):
    return (v, None)

def back_low(kept, grad):
    return (low(grad),)
low.defvjp(low_keep, low_pass)
low_back.defvjp(back_keep, back_low)
HIGH = lax.Precision.HIGHEST
eps = 1e-05
spread = 2.0

def layer_norm(inputs, norm_gain, norm_shift):
    center = lax.optimization_barrier(jnp.mean(inputs, -1, keepdims=True))
    centered = inputs - center
    variance = lax.optimization_barrier(jnp.mean(centered * centered, -1, keepdims=True))
    return centered * lax.rsqrt(variance + eps) * norm_gain + norm_shift

def window_attend(queries, keys_all, values_all):
    padded_keys = jnp.pad(keys_all, ((WIN, WIN), (0, 0), (0, 0)))
    padded_values = jnp.pad(values_all, ((WIN, WIN), (0, 0), (0, 0)))
    begins = (jnp.arange(SEQ_LEN // C) * C).astype(jnp.int32)

    def one_block(begin_at):
        query_block = lax.dynamic_slice_in_dim(queries, begin_at, C, 0)
        key_block = lax.dynamic_slice_in_dim(padded_keys, begin_at, C + 2 * WIN, 0)
        value_block = lax.dynamic_slice_in_dim(padded_values, begin_at, C + 2 * WIN, 0)
        raw_scores = jnp.einsum('qhd,khd->hqk', query_block, key_block, precision=HIGH) * HD ** (-0.5)
        scores = low_back(raw_scores)
        query_at = begin_at + jnp.arange(C)
        key_at = begin_at - WIN + jnp.arange(C + 2 * WIN)
        allowed = (jnp.abs(query_at[:, None] - key_at[None, :]) <= WIN) & (key_at >= 0)[None, :] & (key_at < SEQ_LEN)[None, :]
        scores = jnp.where(allowed[None], scores, -1e+30)
        row_peak = lax.optimization_barrier(jnp.max(scores, -1, keepdims=True))
        weights = jnp.exp(scores - row_peak)
        soft_probs = weights / lax.optimization_barrier(jnp.sum(weights, -1, keepdims=True))
        return jnp.einsum('hqk,khd->qhd', low(soft_probs), value_block, precision=HIGH)
    attended = lax.map(jax.checkpoint(one_block), begins)
    return attended.reshape(SEQ_LEN, H, HD)

def row_forward(parameters, byte_row, length_row, count_row):
    embed_table, gain_one, shift_one, qkv_mat, out_mat, gain_two, shift_two, up_mat, up_vec, down_mat, down_vec, front_vec = parameters
    embedded = embed_table[byte_row]
    normed_one = low(layer_norm(embedded, gain_one, shift_one))
    qkv_rows = low(low_back(jnp.dot(normed_one, qkv_mat, precision=HIGH)))
    queries = qkv_rows[:, :D].reshape(SEQ_LEN, H, HD)
    keys_all = qkv_rows[:, D:2 * D].reshape(SEQ_LEN, H, HD)
    values_all = qkv_rows[:, 2 * D:].reshape(SEQ_LEN, H, HD)
    attended = window_attend(queries, keys_all, values_all).reshape(SEQ_LEN, D)
    attended = low(low_back(attended))
    middle = embedded + low_back(jnp.dot(attended, out_mat, precision=HIGH))
    normed_two = low(layer_norm(middle, gain_two, shift_two))
    preact = low_back(jnp.dot(normed_two, up_mat, precision=HIGH) + up_vec)
    activated = low(jax.nn.gelu(preact, approximate=False))
    hidden = middle + low_back(jnp.dot(activated, down_mat, precision=HIGH) + down_vec)
    frontier = jax.nn.sigmoid(jnp.dot(hidden, front_vec, precision=HIGH))
    in_item = (jnp.arange(SEQ_LEN) < length_row).astype(jnp.float32)
    prob_row = frontier * in_item
    item_total = jnp.sum(prob_row)
    cumulative = jnp.cumsum(prob_row)
    position = count_row.astype(jnp.float32) * cumulative / item_total
    centers = jnp.arange(NB).astype(jnp.float32) + 0.5
    in_block = (jnp.arange(NB) < count_row).astype(jnp.float32)
    distance = position[:, None] - centers[None, :]
    assign = jnp.exp(-spread * distance * distance) * in_item[:, None] * in_block[None, :]
    numer = jnp.dot(assign.T, hidden, precision=HIGH)
    denom = lax.optimization_barrier(jnp.sum(assign, 0))
    return numer / (denom[:, None] + 1.0)

def reference(byte_ids, item_lengths, block_counts, byte_embed, norm1_gain, norm1_shift, qkv_weight, out_weight, norm2_gain, norm2_shift, up_weight, up_bias, down_weight, down_bias, frontier_weight, pooled_cot):
    parameters = tuple((weight.astype(jnp.float32) for weight in (byte_embed, norm1_gain, norm1_shift, qkv_weight, out_weight, norm2_gain, norm2_shift, up_weight, up_bias, down_weight, down_bias, frontier_weight)))

    def per_row(totals, row_data):
        byte_row, length_row, count_row, cot_row = row_data

        def forward(weights):
            return row_forward(weights, byte_row, length_row, count_row)
        pooled_row, backward = jax.vjp(forward, parameters)
        row_grads = backward(cot_row.astype(jnp.float32))[0]
        return (jax.tree.map(jnp.add, totals, row_grads), pooled_row)
    start_totals = jax.tree.map(jnp.zeros_like, parameters)
    grad_sums, pooled = lax.scan(per_row, start_totals, (byte_ids, item_lengths, block_counts, pooled_cot))
    return (pooled, grad_sums[0], grad_sums[1], grad_sums[2], grad_sums[3], grad_sums[4], grad_sums[5], grad_sums[6], grad_sums[7], grad_sums[8], grad_sums[9], grad_sums[10], grad_sums[11])
```

```python
import functools

import jax
import jax.numpy as jnp
from jax import lax
from jax.experimental import pallas as pl
from jax.experimental.pallas import tpu as pltpu
from jax.sharding import PartitionSpec as P

H = 8
HD = 64
WIN = 64
NB = 64
TILE = 128
SPAN_KEYS = TILE + 2 * WIN
PAIR = 2 * HD
STACK = 80

eps = 1e-05
spread = 2.0
LOG2E = 1.4426950408889634
F32 = jnp.float32
BF16 = jnp.bfloat16
VMEM_BYTES = 56 * 1024 * 1024


def dot(left, right):
    return jnp.dot(left, right, preferred_element_type=F32)


def dot_last(left, right):
    return lax.dot_general(left, right, (((1,), (1,)), ((), ())), preferred_element_type=F32)


def dot_first(left, right):
    return lax.dot_general(left, right, (((0,), (0,)), ((), ())), preferred_element_type=F32)


def split_two_outside(value):
    high = lax.reduce_precision(value, 8, 7)
    return high.astype(BF16), (value - high).astype(BF16)


def split_two(value):
    high = value.astype(BF16)
    return high, (value - high.astype(F32)).astype(BF16)


def iota(shape, dim):
    return lax.broadcasted_iota(jnp.int32, shape, dim)


def one_hot_rows(ids_column, vocab):
    cells = iota((ids_column.shape[0], vocab), 1)
    return jnp.where(cells == ids_column, 1.0, 0.0).astype(BF16)


def one_hot_columns(ids_row, vocab):
    cells = iota((vocab, ids_row.shape[1]), 0)
    return jnp.where(cells == ids_row, 1.0, 0.0).astype(BF16)


def gelu_with_slope(value):
    bell = jnp.exp2(value * value * (-0.5 * LOG2E))
    step = 1.0 / (1.0 + jnp.abs(value) * (0.3275911 * 0.7071067811865476))
    series = 0.5 * 1.061405429
    for term in (-1.453152027, 1.421413741, -0.284496736, 0.254829592):
        series = series * step + 0.5 * term
    tail = series * step * bell
    below = jnp.where(value >= 0, 1.0 - tail, tail)
    return value * below, below + value * (bell * 0.3989422804014327)


def window_bias(first, last):
    key_at = iota((SPAN_KEYS, 2 * TILE), 0)
    query_at = iota((SPAN_KEYS, 2 * TILE), 1) & (TILE - 1)
    reach = key_at - query_at
    seen = (reach >= 0) & (reach <= 2 * WIN)
    seen_first = seen & (key_at >= WIN * first)
    seen_last = seen & (key_at < SPAN_KEYS - WIN * last)
    return [jnp.where(kept, 0.0, -1e30) for kept in (seen_first, seen, seen_last)]


def head_blocks(pair_rows):
    lane = iota(pair_rows.shape, 1)
    blank = jnp.zeros_like(pair_rows)
    return jnp.concatenate(
        [jnp.where(lane < HD, pair_rows, blank), jnp.where(lane < HD, blank, pair_rows)], 0
    )


def head_columns(pair_columns):
    return jnp.concatenate([pair_columns[:HD, :TILE], pair_columns[HD:, TILE:]], 0)


def running_sum(row, ones_matrix):
    one, rest = split_two(row)
    high = one.astype(F32) + rest.astype(F32)
    two = (row - high).astype(BF16)
    width = row.shape[1]
    parts = jnp.concatenate([one, rest, two, jnp.zeros((13, width), BF16)], 0)
    sums = dot(parts, ones_matrix)
    return sums[0:1] + sums[1:2] + sums[2:3]


def forward_kernel(
    place, lengths, ids_column, ids_row, table, value_table, embed, out_weight, gain, shift,
    up_weight, up_bias, down_weight, down_bias, cot_stack,
    attended_out, log_out, middle_out, normed_out, act_out, slope_out, high_out, low_out,
    inner_out, frontier_out, running_out,
    bias, query_keys, value_columns, triangle,
):
    item = pl.program_id(0)
    span = middle_out.shape[1]
    model_width = middle_out.shape[2]
    vocab = table.shape[0]
    hidden_width = up_weight.shape[1]

    @pl.when(item == 0)
    def _():
        for at, tile in enumerate(window_bias(place[1], place[2])):
            bias[at] = tile
        triangle[...] = jnp.where(
            iota((span, span), 0) <= iota((span, span), 1), 1.0, 0.0
        ).astype(BF16)

    hot = one_hot_rows(ids_column[0], vocab)
    query_keys[...] = dot(hot, table[...]).astype(BF16)
    value_columns[...] = dot(value_table[...], one_hot_columns(ids_row[0], vocab)).astype(BF16)
    tiles = span // TILE
    for tile in range(tiles):
        begin = tile * TILE
        tile_bias = bias[0 if tile == 0 else (2 if tile == tiles - 1 else 1)]
        for pair in range(H // 2):
            lanes = slice(pair * PAIR, (pair + 1) * PAIR)
            key_lanes = slice(model_width + pair * PAIR, model_width + (pair + 1) * PAIR)
            query_block = head_blocks(query_keys[begin + WIN : begin + WIN + TILE, lanes])
            keys = query_keys[begin : begin + SPAN_KEYS, key_lanes]
            scores = dot_last(keys, query_block) + tile_bias
            peak = jnp.max(scores, 0, keepdims=True)
            weights = jnp.exp(scores - peak)
            weight_sum = jnp.sum(weights, 0, keepdims=True)
            probs = (weights * (1.0 / weight_sum)).astype(BF16)
            mixed = dot(value_columns[lanes, begin : begin + SPAN_KEYS], probs)
            attended_out[0, begin : begin + TILE, lanes] = head_columns(mixed).T.astype(BF16)
            at = tile * (H // 2) + pair
            log_out[0, at : at + 1, :] = peak + jnp.log(weight_sum)
    middle = dot(hot[WIN : WIN + span], embed[...]) + dot(attended_out[0], out_weight[...])
    middle_out[0] = middle
    centered = middle - jnp.mean(middle, -1, keepdims=True)
    variance = jnp.mean(centered * centered, -1, keepdims=True)
    normed = (centered * lax.rsqrt(variance + eps) * gain[...] + shift[...]).astype(BF16)
    normed_out[0] = normed
    chunk = 512
    hidden = middle + down_bias[...]
    for begin in range(0, hidden_width, chunk):
        cells = slice(begin, begin + chunk)
        preact = dot(normed, up_weight[:, cells]) + up_bias[:, cells]
        act, slope = gelu_with_slope(preact)
        act = act.astype(BF16)
        act_out[0, :, cells] = act
        slope_out[0, :, cells] = slope.astype(BF16)
        hidden = hidden + dot(act, down_weight[cells, :])
    high, low = split_two(hidden)
    high_out[0] = high
    low_out[0] = low
    products = dot_last(cot_stack[0, STACK:, :], high)
    inner = products[:STACK] + products[STACK:] + dot_last(cot_stack[0, :STACK, :], low)
    inner_out[0] = inner[:NB]
    frontier = 1.0 / (1.0 + jnp.exp(-inner[NB : NB + 1]))
    frontier_out[0] = frontier
    slot = place[0] + iota((1, span), 1)
    running_out[0] = running_sum(jnp.where(slot < lengths[item], frontier, 0.0), triangle[...])


def assignment(numbers, item, running, slot):
    before, total, count, length = (numbers[item, at] for at in range(4))
    position = count * (running + before) / total
    block_at = iota((NB, running.shape[1]), 0)
    distance = position - (block_at.astype(F32) + 0.5)
    kept = (slot < length) & (block_at.astype(F32) < count)
    assign = jnp.where(kept, jnp.exp(-spread * distance * distance), 0.0)
    return position, assign, assign * distance * (-2.0 * spread)


def pool_kernel(place, numbers, running, inner, high, low, stats_out, numer_out):
    item = pl.program_id(0)
    span = high.shape[1]
    slot = (place[0] + iota((1, span), 1)).astype(F32)
    position, assign, pull = assignment(numbers, item, running[0], slot)
    inner_products = inner[0]
    pull_inner = pull * inner_products
    lane = iota((NB, 128), 1)
    stats = jnp.zeros((NB, 128), F32)
    for at, terms in enumerate(
        (
            assign,
            assign * inner_products,
            pull,
            pull_inner,
            pull * position,
            pull_inner * position,
        )
    ):
        stats = jnp.where(lane == at, jnp.sum(terms, 1, keepdims=True), stats)
    stats_out[0] = stats.T[:8]
    assign_high, assign_low = split_two(assign)
    numer_out[0] = (
        dot(assign_high, high[0]) + dot(assign_low, high[0]) + dot(assign_high, low[0])
    )


def hidden_back_kernel(
    place, numbers, weights, running, frontier, inner, high, low, cot_stack,
    hidden_out, low_out, bias_out, frontier_grad_out,
    triangle,
):
    item = pl.program_id(0)
    span = high.shape[1]

    @pl.when(item == 0)
    def _():
        triangle[...] = jnp.where(
            iota((span, span), 0) >= iota((span, span), 1), 1.0, 0.0
        ).astype(BF16)
        bias_out[...] = jnp.zeros_like(bias_out)
        frontier_grad_out[...] = jnp.zeros_like(frontier_grad_out)

    slot = (place[0] + iota((1, span), 1)).astype(F32)
    position, assign, pull = assignment(numbers, item, running[0], slot)
    inverse = weights[0, :, 0:1]
    d_denom = weights[0, :, 1:2]
    d_position = jnp.sum((inner[0] * inverse + d_denom) * pull, 0, keepdims=True)
    d_cumulative = d_position * numbers[item, 2] / numbers[item, 1]
    d_prob = running_sum(d_cumulative, triangle[...]) + numbers[item, 4]
    share = frontier[0]
    d_logit = jnp.where(slot < numbers[item, 3], d_prob * share * (1.0 - share), 0.0)
    left = jnp.concatenate(
        [assign * inverse, d_logit, jnp.zeros((STACK - NB - 1, span), F32)], 0
    )
    left_high, left_low = split_two(left)
    d_hidden = dot_first(jnp.concatenate([left_high, left_low, left_high], 0), cot_stack[0])
    hidden_out[0] = d_hidden
    d_low = d_hidden.astype(BF16)
    low_out[0] = d_low
    bias_out[...] += jnp.sum(d_low.astype(F32), 0, keepdims=True)
    rows = slice(NB, STACK)
    products = (
        dot(left_high[rows], high[0]) + dot(left_low[rows], high[0]) + dot(left_high[rows], low[0])
    )
    frontier_grad_out[...] += products[0:1]


def feed_back_kernel(
    ids_row, d_hidden, d_hidden_low, slope, middle, gain, down_weight, up_weight, out_weight,
    preact_out, middle_out, attended_out, embed_out, up_bias_out, gain_out, shift_out,
):
    item = pl.program_id(0)
    hidden_width = up_weight.shape[1]
    vocab = embed_out.shape[0]

    @pl.when(item == 0)
    def _():
        for total in (embed_out, up_bias_out, gain_out, shift_out):
            total[...] = jnp.zeros_like(total)

    chunk = 512
    d_normed = None
    for begin in range(0, hidden_width, chunk):
        cells = slice(begin, begin + chunk)
        d_act = dot_last(d_hidden_low[0], down_weight[cells, :])
        d_preact = (d_act * slope[0, :, cells].astype(F32)).astype(BF16)
        preact_out[0, :, cells] = d_preact
        up_bias_out[:, cells] += jnp.sum(d_preact.astype(F32), 0, keepdims=True)
        part = dot_last(d_preact, up_weight[:, cells])
        d_normed = part if d_normed is None else d_normed + part
    rows = middle[0]
    centered = rows - jnp.mean(rows, -1, keepdims=True)
    scale = lax.rsqrt(jnp.mean(centered * centered, -1, keepdims=True) + eps)
    unit = centered * scale
    gain_out[...] += jnp.sum(d_normed * unit, 0, keepdims=True)
    shift_out[...] += jnp.sum(d_normed, 0, keepdims=True)
    pushed = d_normed * gain[...]
    d_middle = d_hidden[0] + scale * (
        pushed
        - jnp.mean(pushed, -1, keepdims=True)
        - unit * jnp.mean(pushed * unit, -1, keepdims=True)
    )
    high, low = split_two(d_middle)
    middle_out[0] = high
    attended_out[0] = dot_last(high, out_weight[...]).astype(BF16)
    hot = one_hot_columns(ids_row[0], vocab)
    embed_out[...] += dot(hot, high) + dot(hot, low)


def attend_back_kernel(
    place, ids_column, ids_row, table, key_table, d_attended, logs,
    queries_out, keys_out, values_out,
    bias, table_rows, key_columns, d_queries, d_keys, d_values, queries_total,
):
    item = pl.program_id(0)
    span = d_attended.shape[1]
    model_width = d_attended.shape[2]
    vocab = table.shape[0]

    @pl.when(item == 0)
    def _():
        for at, tile in enumerate(window_bias(place[1], place[2])):
            bias[at] = tile
        for total in (queries_total, keys_out, values_out):
            total[...] = jnp.zeros_like(total)

    hot = one_hot_rows(ids_column[0], vocab)
    hot_columns = one_hot_columns(ids_row[0], vocab)
    table_rows[...] = dot(hot, table[...]).astype(BF16)
    key_columns[...] = dot(key_table[...], hot_columns).astype(BF16)
    d_keys[...] = jnp.zeros_like(d_keys)
    d_values[...] = jnp.zeros_like(d_values)
    tiles = span // TILE
    for tile in range(tiles):
        begin = tile * TILE
        tile_bias = bias[0 if tile == 0 else (2 if tile == tiles - 1 else 1)]
        window = slice(begin, begin + SPAN_KEYS)
        for pair in range(H // 2):
            lanes = slice(pair * PAIR, (pair + 1) * PAIR)
            key_lanes = slice(model_width + pair * PAIR, model_width + (pair + 1) * PAIR)
            value_lanes = slice(2 * model_width + pair * PAIR, 2 * model_width + (pair + 1) * PAIR)
            query_block = head_blocks(table_rows[begin + WIN : begin + WIN + TILE, lanes])
            grad_block = head_blocks(d_attended[0, begin : begin + TILE, lanes])
            at = tile * (H // 2) + pair
            scores = dot_last(table_rows[window, key_lanes], query_block) + tile_bias
            probs = jnp.exp(scores - logs[0, at : at + 1, :])
            d_probs = dot_last(table_rows[window, value_lanes], grad_block)
            weighted = probs * d_probs
            d_scores = (weighted - probs * jnp.sum(weighted, 0, keepdims=True)).astype(BF16)
            d_values[window, lanes] += dot(probs.astype(BF16), grad_block)
            d_keys[window, lanes] += dot(d_scores, query_block)
            turned = dot(key_columns[lanes, window], d_scores)
            d_queries[lanes, begin : begin + TILE] = (
                head_columns(turned) * (HD**-0.5)
            ).astype(BF16)
    queries_total[...] += dot(d_queries[...], hot[WIN : WIN + span])
    keys_out[...] += dot(hot_columns, d_keys[...].astype(BF16))
    values_out[...] += dot(hot_columns, d_values[...].astype(BF16))

    @pl.when(item == pl.num_programs(0) - 1)
    def _():
        queries_out[...] = queries_total[...].T


def whole(shape):
    return pl.BlockSpec(shape, lambda item: (0,) * len(shape))


def per_item(shape):
    return pl.BlockSpec((1,) + shape, lambda item: (item,) + (0,) * len(shape))


def scalars():
    return pl.BlockSpec(memory_space=pltpu.SMEM)


def call(kernel, items, in_specs, outs, scratch, flops, arrays):
    shapes = [jax.ShapeDtypeStruct(shape, dtype) for _, shape, dtype in outs]
    return pl.pallas_call(
        kernel,
        grid=(items,),
        in_specs=in_specs,
        out_specs=[spec for spec, _, _ in outs],
        out_shape=shapes,
        scratch_shapes=scratch,
        compiler_params=pltpu.CompilerParams(vmem_limit_bytes=VMEM_BYTES),
        cost_estimate=pl.CostEstimate(
            flops=flops,
            bytes_accessed=sum(
                cells.size * cells.dtype.itemsize for cells in list(arrays) + shapes
            ),
            transcendentals=0,
        ),
    )(*arrays)


def item_out(items, shape, dtype):
    return per_item(shape), (items,) + shape, dtype


def total_out(shape, dtype=F32):
    return whole(shape), shape, dtype


def bits_of(count):
    return [1 << at for at in range(count.bit_length() - 1)]


def scan_over(axis, cells, index):
    count = lax.axis_size(axis)
    earlier = jnp.zeros_like(cells)
    later = jnp.zeros_like(cells)
    for bit in bits_of(count):
        other = lax.ppermute(cells, axis, [(at, at ^ bit) for at in range(count)])
        upper = (index & bit) != 0
        earlier = earlier + jnp.where(upper, other, 0.0)
        later = later + jnp.where(upper, 0.0, other)
        cells = cells + other
    return earlier, cells, later


class Exchange:
    def __init__(self):
        self.outer = lax.axis_size("dp")
        self.inner = lax.axis_size("seq")
        outer_bits = [("dp", bit) for bit in bits_of(self.outer)]
        inner_bits = [("seq", bit) for bit in bits_of(self.inner)]
        rest = outer_bits[1:] + inner_bits[:-1]
        turn = len(outer_bits) - 1
        first = outer_bits[:1]
        last = inner_bits[-1:]
        self.orders = (first + rest + last, first + rest[turn:] + rest[:turn] + last)
        self.steps = len(self.orders[0])
        self.at = {"dp": lax.axis_index("dp"), "seq": lax.axis_index("seq")}

    def partner(self, flat, step):
        outer, inner = divmod(flat, self.inner)
        axis, bit = self.orders[outer & 1][step]
        if axis == "dp":
            outer ^= bit
        else:
            inner ^= bit
        return outer * self.inner + inner

    def swap(self, cells, step):
        devices = self.outer * self.inner
        pairs = [(flat, self.partner(flat, step)) for flat in range(devices)]
        return lax.ppermute(cells, ("dp", "seq"), pairs)

    def side(self, step):
        picked = [
            ((self.at[axis] & bit) != 0).astype(jnp.int32)
            for axis, bit in (order[step] for order in self.orders)
        ]
        return jnp.where((self.at["dp"] & 1) == 0, picked[0], picked[1])

    def scatter_sum(self, cells, extra=None):
        for step in range(self.steps):
            half = cells.shape[0] // 2
            side = self.side(step)
            sent = lax.dynamic_slice_in_dim(cells, (1 - side) * half, half, 0)
            kept = lax.dynamic_slice_in_dim(cells, side * half, half, 0)
            if extra is not None:
                high, low = split_two_outside(extra)
                sent = jnp.concatenate([sent, high, low], 0)
            came = self.swap(sent, step)
            cells = (kept.astype(F32) + came[:half].astype(F32)).astype(BF16)
            if extra is not None:
                rows = extra.shape[0]
                mine = high.astype(F32) + low.astype(F32)
                extra = mine + (
                    came[half : half + rows].astype(F32) + came[half + rows :].astype(F32)
                )
        return cells, extra

    def gather(self, cells):
        for step in reversed(range(self.steps)):
            side = self.side(step)
            came = self.swap(cells, step)
            half = cells.shape[0]
            joined = jnp.zeros((2 * half,) + cells.shape[1:], cells.dtype)
            joined = lax.dynamic_update_slice_in_dim(joined, cells, side * half, 0)
            cells = lax.dynamic_update_slice_in_dim(joined, came, (1 - side) * half, 0)
        return cells


def local(
    byte_ids,
    item_lengths,
    block_counts,
    byte_embed,
    norm1_gain,
    norm1_shift,
    qkv_weight,
    out_weight,
    norm2_gain,
    norm2_shift,
    up_weight,
    up_bias,
    down_weight,
    down_bias,
    frontier_weight,
    pooled_cot,
):
    items, span = byte_ids.shape
    vocab, model_width = byte_embed.shape
    hidden_width = up_weight.shape[1]
    seq_count = lax.axis_size("seq")
    seq_place = lax.axis_index("seq")
    tokens = items * span
    wide = span + 2 * WIN
    tiles = span // TILE

    ends = range(seq_count - 1)
    ids_wide = jnp.concatenate(
        [
            lax.ppermute(byte_ids[:, span - WIN :], "seq", [(at, at + 1) for at in ends]),
            byte_ids,
            lax.ppermute(byte_ids[:, :WIN], "seq", [(at + 1, at) for at in ends]),
        ],
        1,
    )
    ids_column = ids_wide[:, :, None]
    ids_row = ids_wide[:, None, :]

    embed_rows = byte_embed.astype(F32)
    centered = embed_rows - jnp.mean(embed_rows, -1, keepdims=True)
    scale_one = lax.rsqrt(jnp.mean(centered * centered, -1, keepdims=True) + eps)
    unit_one = centered * scale_one
    normed_one = (unit_one * norm1_gain + norm1_shift).astype(BF16)
    table = dot(normed_one, qkv_weight).astype(BF16)
    query_scale = jnp.where(jnp.arange(3 * model_width) < model_width, HD**-0.5, 1.0).astype(BF16)
    scaled_table = table * query_scale
    key_table = table[:, model_width : 2 * model_width].T
    value_table = table[:, 2 * model_width :].T

    cot_rows = jnp.concatenate(
        [
            pooled_cot,
            jnp.broadcast_to(frontier_weight, (items, 1, model_width)),
            jnp.zeros((items, STACK - NB - 1, model_width), F32),
        ],
        1,
    )
    cot_high, cot_low = split_two_outside(cot_rows)
    cot_stack = jnp.concatenate([cot_high, cot_high, cot_low], 1)

    first = (seq_place == 0).astype(jnp.int32)
    last = (seq_place == seq_count - 1).astype(jnp.int32)
    place = jnp.stack([seq_place * span, first, last]).astype(jnp.int32)

    square = (span, model_width)
    full = (span, hidden_width)
    row = (1, span)
    (
        attended, logs, middle, normed_two, act, slope, hidden_high, hidden_low,
        inner, frontier, running,
    ) = call(
        forward_kernel,
        items,
        [scalars(), scalars(), per_item((wide, 1)), per_item((1, wide))]
        + [
            whole(shape)
            for shape in (
                (vocab, 2 * model_width), (model_width, vocab), (vocab, model_width),
                (model_width, model_width), (1, model_width), (1, model_width),
                (model_width, hidden_width), (1, hidden_width),
                (hidden_width, model_width), (1, model_width),
            )
        ]
        + [per_item((3 * STACK, model_width))],
        [
            item_out(items, square, BF16),
            item_out(items, (tiles * H // 2, 2 * TILE), F32),
            item_out(items, square, F32),
            item_out(items, square, BF16),
            item_out(items, full, BF16),
            item_out(items, full, BF16),
            item_out(items, square, BF16),
            item_out(items, square, BF16),
            item_out(items, (NB, span), F32),
            item_out(items, row, F32),
            item_out(items, row, F32),
        ],
        [
            pltpu.VMEM((3, SPAN_KEYS, 2 * TILE), F32),
            pltpu.VMEM((wide, 2 * model_width), BF16),
            pltpu.VMEM((model_width, wide), BF16),
            pltpu.VMEM((span, span), BF16),
        ],
        2 * tokens * model_width * (2 * hidden_width + 3 * model_width),
        (
            place, item_lengths, ids_column, ids_row, scaled_table[:, : 2 * model_width],
            value_table, byte_embed, out_weight, norm2_gain[None], norm2_shift[None],
            up_weight, up_bias[None], down_weight, down_bias[None], cot_stack,
        ),
    )

    mass = running[:, 0, span - 1]
    mass_before, item_total, _ = scan_over("seq", mass, seq_place)
    counts_real = block_counts.astype(F32)
    lengths_real = item_lengths.astype(F32)
    numbers = jnp.stack([mass_before, item_total, counts_real, lengths_real], 1)

    stats, numer = call(
        pool_kernel,
        items,
        [scalars(), scalars(), per_item(row), per_item((NB, span)), per_item(square), per_item(square)],
        [item_out(items, (8, NB), F32), item_out(items, (NB, model_width), F32)],
        [],
        6 * tokens * NB * model_width,
        (place, numbers, running, inner, hidden_high, hidden_low),
    )

    _, stats_whole, stats_after = scan_over("seq", stats, seq_place)
    inverse = 1.0 / (stats_whole[:, 0] + 1.0)
    d_denom = -inverse * inverse * stats_whole[:, 1]
    pooled = lax.psum(numer, "seq") * inverse[:, :, None]
    push_after = jnp.sum(d_denom * stats_after[:, 2] + inverse * stats_after[:, 3], 1)
    total_sum = jnp.sum(d_denom * stats_whole[:, 4] + inverse * stats_whole[:, 5], 1)
    constant = (push_after * counts_real - total_sum) / item_total
    numbers_back = jnp.concatenate([numbers, constant[:, None]], 1)
    block_weights = jnp.stack([inverse, d_denom], 2)

    d_hidden, d_hidden_low, d_down_bias, d_frontier = call(
        hidden_back_kernel,
        items,
        [scalars(), scalars(), per_item((NB, 2)), per_item(row), per_item(row), per_item((NB, span)),
         per_item(square), per_item(square), per_item((3 * STACK, model_width))],
        [
            item_out(items, square, F32),
            item_out(items, square, BF16),
            total_out((1, model_width)),
            total_out((1, model_width)),
        ],
        [pltpu.VMEM((span, span), BF16)],
        8 * tokens * NB * model_width,
        (place, numbers_back, block_weights, running, frontier, inner, hidden_high, hidden_low,
         cot_stack),
    )
    flat_act = act.reshape(tokens, hidden_width)
    d_down = dot_first(flat_act, d_hidden_low.reshape(tokens, model_width)).astype(BF16)

    (
        d_preact, d_middle, d_attended, d_embed_direct, d_up_bias, d_gain_two, d_shift_two,
    ) = call(
        feed_back_kernel,
        items,
        [per_item(row), per_item(square), per_item(square), per_item(full), per_item(square),
         whole((1, model_width)), whole((hidden_width, model_width)),
         whole((model_width, hidden_width)), whole((model_width, model_width))],
        [
            item_out(items, full, BF16),
            item_out(items, square, BF16),
            item_out(items, square, BF16),
            total_out((vocab, model_width)),
            total_out((1, hidden_width)),
            total_out((1, model_width)),
            total_out((1, model_width)),
        ],
        [],
        4 * tokens * model_width * hidden_width,
        (byte_ids[:, None, :], d_hidden, d_hidden_low, slope, middle, norm2_gain[None],
         down_weight, up_weight, out_weight),
    )
    d_up = dot_first(
        normed_two.reshape(tokens, model_width), d_preact.reshape(tokens, hidden_width)
    ).astype(BF16)
    d_out = dot_first(
        attended.reshape(tokens, model_width), d_middle.reshape(tokens, model_width)
    ).astype(BF16)

    d_queries, d_keys, d_values = call(
        attend_back_kernel,
        items,
        [scalars(), per_item((wide, 1)), per_item((1, wide)), whole((vocab, 3 * model_width)),
         whole((model_width, vocab)), per_item(square), per_item((tiles * H // 2, 2 * TILE))],
        [total_out((vocab, model_width))] * 3,
        [
            pltpu.VMEM((3, SPAN_KEYS, 2 * TILE), F32),
            pltpu.VMEM((wide, 3 * model_width), BF16),
            pltpu.VMEM((model_width, wide), BF16),
            pltpu.VMEM((model_width, span), BF16),
            pltpu.VMEM((wide, model_width), F32),
            pltpu.VMEM((wide, model_width), F32),
            pltpu.VMEM((model_width, vocab), F32),
        ],
        10 * tokens * SPAN_KEYS * model_width,
        (place, ids_column, ids_row, scaled_table, key_table, d_attended, logs),
    )

    exchange = Exchange()
    blocks = hidden_width // model_width
    big = jnp.concatenate(
        [d_down]
        + [d_up[:, at * model_width : (at + 1) * model_width] for at in range(blocks)]
        + [d_out],
        0,
    )
    small = jnp.concatenate(
        [d_embed_direct.astype(BF16), d_queries.astype(BF16), d_keys.astype(BF16),
         d_values.astype(BF16)],
        0,
    )
    vectors = jnp.concatenate(
        [d_gain_two, d_shift_two, d_down_bias, d_frontier,
         d_up_bias.reshape(blocks, model_width)],
        0,
    )
    big_share, _ = exchange.scatter_sum(big)
    small_share, vectors = exchange.scatter_sum(small, vectors)
    big = exchange.gather(big_share).astype(F32)
    small = exchange.gather(small_share)

    d_down = big[:hidden_width]
    d_up = jnp.concatenate(
        [
            big[hidden_width + at * model_width : hidden_width + (at + 1) * model_width]
            for at in range(blocks)
        ],
        1,
    )
    d_out = big[2 * hidden_width :]
    d_table = jnp.concatenate(
        [small[at * vocab : (at + 1) * vocab] for at in range(1, 4)], 1
    )
    d_qkv = dot_first(normed_one, d_table)
    d_normed_one = dot_last(d_table, qkv_weight)
    d_gain_one = jnp.sum(d_normed_one * unit_one, 0)
    d_shift_one = jnp.sum(d_normed_one, 0)
    pushed = d_normed_one * norm1_gain
    d_embed = small[:vocab].astype(F32) + scale_one * (
        pushed
        - jnp.mean(pushed, -1, keepdims=True)
        - unit_one * jnp.mean(pushed * unit_one, -1, keepdims=True)
    )
    return (
        pooled,
        d_embed,
        d_gain_one,
        d_shift_one,
        d_qkv,
        d_out,
        vectors[0],
        vectors[1],
        d_up,
        vectors[4:].reshape(-1),
        d_down,
        vectors[2],
        vectors[3],
    )


def solution(mesh):
    placed = (P("dp", "seq"), P("dp"), P("dp")) + (P(),) * 12 + (P("dp", None, None),)
    return jax.shard_map(
        local,
        mesh=mesh,
        in_specs=placed,
        out_specs=(P("dp", None, None),) + (P(),) * 12,
        check_vma=False,
    )
```

```python
import functools

import jax
import jax.numpy as jnp
from jax import lax
from jax.experimental import pallas as pl
from jax.experimental.pallas import tpu as pltpu
from jax.sharding import PartitionSpec as P

H = 8
HD = 64
WIN = 64
NB = 64
TILE = 128
SPAN_KEYS = TILE + 2 * WIN
PAIR = 2 * HD
STACK = 80

eps = 1e-05
spread = 2.0
LOG2E = 1.4426950408889634
F32 = jnp.float32
BF16 = jnp.bfloat16
VMEM_BYTES = 56 * 1024 * 1024


def dot(left, right):
    return jnp.dot(left, right, preferred_element_type=F32)


def dot_last(left, right):
    return lax.dot_general(left, right, (((1,), (1,)), ((), ())), preferred_element_type=F32)


def dot_first(left, right):
    return lax.dot_general(left, right, (((0,), (0,)), ((), ())), preferred_element_type=F32)


def split_two_outside(value):
    high = lax.reduce_precision(value, 8, 7)
    return high.astype(BF16), (value - high).astype(BF16)


def split_two(value):
    high = value.astype(BF16)
    return high, (value - high.astype(F32)).astype(BF16)


def iota(shape, dim):
    return lax.broadcasted_iota(jnp.int32, shape, dim)


def one_hot_columns(ids_row, vocab):
    cells = iota((vocab, ids_row.shape[1]), 0)
    return jnp.where(cells == ids_row, 1.0, 0.0).astype(BF16)


def gelu_with_slope(value):
    below = 0.5 + 0.5 * lax.erf(value * 0.7071067811865476)
    bell = jnp.exp2(value * value * (-0.5 * LOG2E))
    return value * below, below + value * (bell * 0.3989422804014327)


def window_bias(first, last):
    key_at = iota((SPAN_KEYS, 2 * TILE), 0)
    query_at = iota((SPAN_KEYS, 2 * TILE), 1) & (TILE - 1)
    reach = key_at - query_at
    seen = (reach >= 0) & (reach <= 2 * WIN)
    seen_first = seen & (key_at >= WIN * first)
    seen_last = seen & (key_at < SPAN_KEYS - WIN * last)
    return [jnp.where(kept, 0.0, -1e30) for kept in (seen_first, seen, seen_last)]


def head_blocks(pair_rows):
    lane = iota(pair_rows.shape, 1)
    blank = jnp.zeros_like(pair_rows)
    return jnp.concatenate(
        [jnp.where(lane < HD, pair_rows, blank), jnp.where(lane < HD, blank, pair_rows)], 0
    )


def head_columns(pair_columns):
    return jnp.concatenate([pair_columns[:HD, :TILE], pair_columns[HD:, TILE:]], 0)


def running_sum(row, ones_matrix):
    one, rest = split_two(row)
    high = one.astype(F32) + rest.astype(F32)
    two = (row - high).astype(BF16)
    width = row.shape[1]
    parts = jnp.concatenate([one, rest, two, jnp.zeros((13, width), BF16)], 0)
    sums = dot(parts, ones_matrix)
    return sums[0:1] + sums[1:2] + sums[2:3]


def table_kernel(
    embed, gain, shift, weight, cot, frontier_weight,
    normed_out, table_out, key_out, value_out, stack_out,
):
    rows = embed[...].astype(F32)
    centered = rows - jnp.mean(rows, -1, keepdims=True)
    scale = lax.rsqrt(jnp.mean(centered * centered, -1, keepdims=True) + eps)
    normed = (centered * scale * gain[...] + shift[...]).astype(BF16)
    normed_out[...] = normed
    model_width = rows.shape[1]
    table = dot(normed, weight[...])
    queries = table[:, :model_width].astype(BF16).astype(F32) * HD**-0.5
    table_out[:, :model_width] = queries.astype(BF16)
    table_out[:, model_width:] = table[:, model_width:].astype(BF16)
    key_out[...] = table[:, model_width : 2 * model_width].T.astype(BF16)
    value_out[...] = table[:, 2 * model_width :].T.astype(BF16)
    rim_high, rim_low = split_two(
        jnp.where(iota((STACK - NB, model_width), 0) == 0, frontier_weight[...], 0.0)
    )
    for item in range(cot.shape[0]):
        high, low = split_two(cot[item])
        for at, (block, rim) in enumerate(((high, rim_high), (high, rim_high), (low, rim_low))):
            stack_out[item, at * STACK : at * STACK + NB] = block
            stack_out[item, at * STACK + NB : (at + 1) * STACK] = rim


def forward_kernel(
    place, lengths, ids_row, table, value_table, embed, out_weight, gain, shift,
    up_weight, up_bias, down_weight, down_bias, cot_stack,
    attended_out, log_out, middle_out, normed_out, act_out, slope_out, high_out, low_out,
    inner_out, frontier_out, running_out,
    bias, query_keys, value_columns, triangle,
):
    item = pl.program_id(0)
    span = middle_out.shape[1]
    model_width = middle_out.shape[2]
    vocab = embed.shape[0]
    hidden_width = up_weight.shape[1]

    @pl.when(item == 0)
    def _():
        for at, tile in enumerate(window_bias(place[1], place[2])):
            bias[at] = tile
        triangle[...] = jnp.where(
            iota((span, span), 0) <= iota((span, span), 1), 1.0, 0.0
        ).astype(BF16)

    hot_columns = one_hot_columns(ids_row[0], vocab)
    hot = hot_columns.T
    query_keys[...] = dot(hot, table[:, : 2 * model_width]).astype(BF16)
    value_columns[...] = dot(value_table[...], hot_columns).astype(BF16)
    tiles = span // TILE
    pairs = H // 2
    for tile in range(tiles):
        begin = tile * TILE
        window = slice(begin, begin + SPAN_KEYS)
        tile_bias = bias[0 if tile == 0 else (2 if tile == tiles - 1 else 1)]
        lanes = [slice(pair * PAIR, (pair + 1) * PAIR) for pair in range(pairs)]
        scores = []
        for pair in range(pairs):
            key_lanes = slice(model_width + pair * PAIR, model_width + (pair + 1) * PAIR)
            query_block = head_blocks(query_keys[begin + WIN : begin + WIN + TILE, lanes[pair]])
            scores.append(dot_last(query_keys[window, key_lanes], query_block) + tile_bias)
        probs = []
        for pair in range(pairs):
            peak = jnp.max(scores[pair], 0, keepdims=True)
            weights = jnp.exp(scores[pair] - peak)
            weight_sum = jnp.sum(weights, 0, keepdims=True)
            probs.append((weights * pltpu.reciprocal(weight_sum, approx=True)).astype(BF16))
            at = tile * pairs + pair
            log_out[0, at : at + 1, :] = peak + jnp.log(weight_sum)
        mixed = [dot(value_columns[lanes[pair], window], probs[pair]) for pair in range(pairs)]
        for pair in range(pairs):
            attended_out[0, begin : begin + TILE, lanes[pair]] = (
                head_columns(mixed[pair]).T.astype(BF16)
            )
    middle = dot(hot[WIN : WIN + span], embed[...]) + dot(attended_out[0], out_weight[...])
    middle_out[0] = middle
    centered = middle - jnp.mean(middle, -1, keepdims=True)
    variance = jnp.mean(centered * centered, -1, keepdims=True)
    normed = (centered * lax.rsqrt(variance + eps) * gain[...] + shift[...]).astype(BF16)
    normed_out[0] = normed
    chunk = 512
    cuts = [slice(begin, begin + chunk) for begin in range(0, hidden_width, chunk)]
    hidden = middle + down_bias[...]
    preact = dot(normed, up_weight[:, cuts[0]]) + up_bias[:, cuts[0]]
    for at, cells in enumerate(cuts):
        held = preact
        if at + 1 < len(cuts):
            preact = dot(normed, up_weight[:, cuts[at + 1]]) + up_bias[:, cuts[at + 1]]
        act, slope = gelu_with_slope(held)
        act = act.astype(BF16)
        act_out[0, :, cells] = act
        slope_out[0, :, cells] = slope.astype(BF16)
        hidden = hidden + dot(act, down_weight[cells, :])
    high, low = split_two(hidden)
    high_out[0] = high
    low_out[0] = low
    products = dot_last(cot_stack[0, STACK:, :], high)
    inner = products[:STACK] + products[STACK:] + dot_last(cot_stack[0, :STACK, :], low)
    inner_out[0] = inner[:NB]
    frontier = 1.0 / (1.0 + jnp.exp(-inner[NB : NB + 1]))
    frontier_out[0] = frontier
    slot = place[0] + iota((1, span), 1)
    running_out[0] = running_sum(jnp.where(slot < lengths[item], frontier, 0.0), triangle[...])


def assignment(place, lengths, counts, before, total, running):
    item = pl.program_id(0)
    span = running.shape[2]
    slot = place[0] + iota((1, span), 1)
    inside = slot < lengths[item]
    count = counts[item].astype(F32)
    position = count * (running[0] + before[item]) / total[item]
    block_at = iota((NB, span), 0)
    distance = position - (block_at.astype(F32) + 0.5)
    kept = inside & (block_at < counts[item])
    assign = jnp.where(kept, jnp.exp(-spread * distance * distance), 0.0)
    return position, assign, assign * distance * (-2.0 * spread), inside, count


def stats_kernel(place, lengths, counts, before, total, running, inner, stats_out):
    position, assign, pull, _, _ = assignment(place, lengths, counts, before, total, running)
    pull_inner = pull * inner[0]
    lane = iota((NB, 128), 1)
    stats = jnp.zeros((NB, 128), F32)
    terms = (
        assign, assign * inner[0], pull, pull_inner, pull * position, pull_inner * position,
    )
    for at, cells in enumerate(terms):
        stats = jnp.where(lane == at, jnp.sum(cells, 1, keepdims=True), stats)
    stats_out[0] = stats.T[:8]


def numer_kernel(place, lengths, counts, before, total, running, high, low, numer_out):
    _, assign, _, _, _ = assignment(place, lengths, counts, before, total, running)
    assign_high, assign_low = split_two(assign)
    numer_out[0] = (
        dot(assign_high, high[0]) + dot(assign_low, high[0]) + dot(assign_high, low[0])
    )


def hidden_gradient(
    place, lengths, counts, before, total, running, frontier, inner, whole_stats, after_stats,
    triangle,
):
    item = pl.program_id(0)
    span = running.shape[2]
    position, assign, pull, inside, count = assignment(
        place, lengths, counts, before, total, running
    )
    whole_columns = whole_stats[0].T
    after_columns = after_stats[0].T
    inverse = 1.0 / (whole_columns[:, 0:1] + 1.0)
    d_denom = -inverse * inverse * whole_columns[:, 1:2]
    push = jnp.sum(
        d_denom * after_columns[:, 2:3] + inverse * after_columns[:, 3:4], 0, keepdims=True
    )
    pushed = jnp.sum(
        d_denom * whole_columns[:, 4:5] + inverse * whole_columns[:, 5:6], 0, keepdims=True
    )
    d_position = jnp.sum((inner[0] * inverse + d_denom) * pull, 0, keepdims=True)
    d_cumulative = d_position * count / total[item]
    d_prob = running_sum(d_cumulative, triangle[...]) + (push * count - pushed) / total[item]
    share = frontier[0]
    d_logit = jnp.where(inside, d_prob * share * (1.0 - share), 0.0)
    left = jnp.concatenate(
        [assign * inverse, d_logit, jnp.zeros((STACK - NB - 1, span), F32)], 0
    )
    return split_two(left)


def write_halves(place, total, sent_out, kept_out):
    half = kept_out.shape[0]
    core = place[3]
    sent_out[...] = total[pl.ds(pl.multiple_of((1 - core) * half, half), half)].astype(BF16)
    kept_out[...] = total[pl.ds(pl.multiple_of(core * half, half), half)].astype(BF16)


def suffix_ones(triangle):
    triangle[...] = jnp.where(
        iota(triangle.shape, 0) >= iota(triangle.shape, 1), 1.0, 0.0
    ).astype(BF16)


def back_kernel(
    place, lengths, counts, before, total, running, frontier, inner, whole_stats, after_stats,
    cot_stack, ids_row, act, slope, high, low, middle, normed, attended, gain, down_weight,
    up_weight, out_weight,
    down_sent, down_kept, up_sent, up_kept, attended_out, embed_out, rows_out,
    triangle, down_total, up_total,
):
    hidden_width = up_weight.shape[1]
    model_width = up_weight.shape[0]
    vocab = embed_out.shape[0]

    @pl.when(pl.program_id(0) == 0)
    def _():
        suffix_ones(triangle)
        for cells in (down_total, up_total, embed_out, rows_out):
            cells[...] = jnp.zeros_like(cells)

    left_high, left_low = hidden_gradient(
        place, lengths, counts, before, total, running, frontier, inner, whole_stats,
        after_stats, triangle,
    )
    d_hidden = dot_first(jnp.concatenate([left_high, left_low, left_high], 0), cot_stack[0])
    d_low = d_hidden.astype(BF16)
    cuts = [
        slice(begin, begin + model_width) for begin in range(0, hidden_width, model_width)
    ]
    d_act = dot_last(d_low, down_weight[cuts[0], :])
    d_normed = None
    for at, cells in enumerate(cuts):
        held = d_act
        if at + 1 < len(cuts):
            d_act = dot_last(d_low, down_weight[cuts[at + 1], :])
        d_preact = (held * slope[0, :, cells].astype(F32)).astype(BF16)
        down_total[cells, :] += dot_first(act[0, :, cells], d_low)
        part = dot_last(d_preact, up_weight[:, cells])
        d_normed = part if d_normed is None else d_normed + part
        up_total[cells, :] += dot_first(normed[0], d_preact)
        rows_out[4 + at : 5 + at] += jnp.sum(d_preact.astype(F32), 0, keepdims=True)
    rows = middle[0]
    centered = rows - jnp.mean(rows, -1, keepdims=True)
    scale = lax.rsqrt(jnp.mean(centered * centered, -1, keepdims=True) + eps)
    unit = centered * scale
    tail = slice(NB, STACK)
    products = (
        dot(left_high[tail], high[0]) + dot(left_low[tail], high[0]) + dot(left_high[tail], low[0])
    )
    rows_out[2:3] += jnp.sum(d_low.astype(F32), 0, keepdims=True)
    rows_out[3:4] += products[0:1]
    rows_out[0:1] += jnp.sum(d_normed * unit, 0, keepdims=True)
    rows_out[1:2] += jnp.sum(d_normed, 0, keepdims=True)
    pushed = d_normed * gain[...]
    d_middle = d_hidden + scale * (
        pushed
        - jnp.mean(pushed, -1, keepdims=True)
        - unit * jnp.mean(pushed * unit, -1, keepdims=True)
    )
    middle_high, middle_low = split_two(d_middle)
    attended_out[0] = dot_last(middle_high, out_weight[...]).astype(BF16)
    up_total[hidden_width:, :] += dot_first(attended[0], middle_high)
    hot = one_hot_columns(ids_row[0], vocab)
    embed_out[...] += dot(hot, middle_high) + dot(hot, middle_low)

    @pl.when(pl.program_id(0) == pl.num_programs(0) - 1)
    def _():
        write_halves(place, down_total, down_sent, down_kept)
        write_halves(place, up_total, up_sent, up_kept)


def attend_back_kernel(
    place, ids_row, table, key_table, d_attended, logs, rows_in,
    *outs_and_scratch,
):
    *outs, rows_total, bias, table_rows, key_columns, d_queries, d_keys, d_values, (
        queries_total
    ) = outs_and_scratch
    item = pl.program_id(0)
    span = d_attended.shape[1]
    model_width = d_attended.shape[2]
    vocab = table.shape[0]

    @pl.when(item == 0)
    def _():
        for at, tile in enumerate(window_bias(place[1], place[2])):
            bias[at] = tile
        given = rows_in.shape[0]
        rows_total[:given] = rows_in[...]
        if given < 4 * vocab:
            rows_total[given:] = jnp.zeros((4 * vocab - given, model_width), F32)
        queries_total[...] = jnp.zeros_like(queries_total)

    hot_columns = one_hot_columns(ids_row[0], vocab)
    hot = hot_columns.T
    table_rows[...] = dot(hot, table[...]).astype(BF16)
    key_columns[...] = dot(key_table[...], hot_columns).astype(BF16)
    d_keys[...] = jnp.zeros_like(d_keys)
    d_values[...] = jnp.zeros_like(d_values)
    tiles = span // TILE
    pairs = H // 2
    for tile in range(tiles):
        begin = tile * TILE
        tile_bias = bias[0 if tile == 0 else (2 if tile == tiles - 1 else 1)]
        window = slice(begin, begin + SPAN_KEYS)
        lanes = [slice(pair * PAIR, (pair + 1) * PAIR) for pair in range(pairs)]
        query_blocks, grad_blocks, scores, d_probs = [], [], [], []
        for pair in range(pairs):
            key_lanes = slice(model_width + pair * PAIR, model_width + (pair + 1) * PAIR)
            value_lanes = slice(2 * model_width + pair * PAIR, 2 * model_width + (pair + 1) * PAIR)
            query_blocks.append(
                head_blocks(table_rows[begin + WIN : begin + WIN + TILE, lanes[pair]])
            )
            grad_blocks.append(head_blocks(d_attended[0, begin : begin + TILE, lanes[pair]]))
            scores.append(dot_last(table_rows[window, key_lanes], query_blocks[pair]) + tile_bias)
            d_probs.append(dot_last(table_rows[window, value_lanes], grad_blocks[pair]))
        probs_low, d_scores = [], []
        for pair in range(pairs):
            at = tile * pairs + pair
            probs = jnp.exp(scores[pair] - logs[0, at : at + 1, :])
            weighted = probs * d_probs[pair]
            probs_low.append(probs.astype(BF16))
            d_scores.append(
                (weighted - probs * jnp.sum(weighted, 0, keepdims=True)).astype(BF16)
            )
        for pair in range(pairs):
            d_values[window, lanes[pair]] += dot(probs_low[pair], grad_blocks[pair])
            d_keys[window, lanes[pair]] += dot(d_scores[pair], query_blocks[pair])
        turned = [dot(key_columns[lanes[pair], window], d_scores[pair]) for pair in range(pairs)]
        for pair in range(pairs):
            d_queries[lanes[pair], begin : begin + TILE] = (
                head_columns(turned[pair]) * (HD**-0.5)
            ).astype(BF16)
    queries_total[...] += dot(d_queries[...], hot[WIN : WIN + span])
    rows_total[2 * vocab : 3 * vocab] += dot(hot_columns, d_keys[...].astype(BF16))
    rows_total[3 * vocab :] += dot(hot_columns, d_values[...].astype(BF16))

    @pl.when(item == pl.num_programs(0) - 1)
    def _():
        rows_total[vocab : 2 * vocab] += queries_total[...].T
        if len(outs) == 2:
            write_halves(place, rows_total, *outs)
        else:
            outs[0][...] = rows_total[...]


def whole(shape):
    return pl.BlockSpec(shape, lambda item: (0,) * len(shape))


def per_item(shape):
    return pl.BlockSpec((1,) + shape, lambda item: (item,) + (0,) * len(shape))


def item_from(shape, first):
    return pl.BlockSpec((1,) + shape, lambda item: (item + first,) + (0,) * len(shape))


def scalars():
    return pl.BlockSpec(memory_space=pltpu.SMEM)


def call(kernel, items, in_specs, outs, scratch, flops, arrays):
    flops = 1
    shapes = [jax.ShapeDtypeStruct(shape, dtype) for _, shape, dtype in outs]
    return pl.pallas_call(
        kernel,
        grid=(items,),
        in_specs=in_specs,
        out_specs=[spec for spec, _, _ in outs],
        out_shape=shapes,
        scratch_shapes=scratch,
        compiler_params=pltpu.CompilerParams(vmem_limit_bytes=VMEM_BYTES),
        cost_estimate=pl.CostEstimate(flops=flops, bytes_accessed=0, transcendentals=0),
    )(*arrays)


def item_out(items, shape, dtype):
    return per_item(shape), (items,) + shape, dtype


def halves_out(rows, width):
    return [total_out((rows // 2, width), BF16)] * 2


def total_out(shape, dtype=F32):
    return whole(shape), shape, dtype


def bits_of(count):
    return [1 << at for at in range(count.bit_length() - 1)]


def scan_over(axis, cells, index, beside=None):
    count = lax.axis_size(axis)
    earlier = jnp.zeros_like(cells)
    later = jnp.zeros_like(cells)
    for step, bit in enumerate(bits_of(count)):
        if step == 1 and beside is not None:
            cells, beside = lax.optimization_barrier((cells, beside))
        other = lax.ppermute(cells, axis, [(at, at ^ bit) for at in range(count)])
        upper = (index & bit) != 0
        earlier = earlier + jnp.where(upper, other, 0.0)
        later = later + jnp.where(upper, 0.0, other)
        cells = cells + other
    return earlier, cells, later, beside


def all_sum(axis, cells):
    count = lax.axis_size(axis)
    index = lax.axis_index(axis)
    steps = [
        (((index & bit) != 0).astype(jnp.int32), [(at, at ^ bit) for at in range(count)])
        for bit in bits_of(count)
    ]
    for side, pairs in steps:
        half = cells.shape[0] // 2
        sent = lax.dynamic_slice_in_dim(cells, (1 - side) * half, half, 0).astype(BF16)
        kept = lax.dynamic_slice_in_dim(cells, side * half, half, 0)
        cells = kept + lax.ppermute(sent, axis, pairs).astype(F32)
    cells = cells.astype(BF16)
    for side, pairs in reversed(steps):
        cells = joined(cells, lax.ppermute(cells, axis, pairs), side)
    return cells.astype(F32)


def joined(mine, came, side):
    half = mine.shape[0]
    cells = jnp.zeros((2 * half,) + mine.shape[1:], mine.dtype)
    cells = lax.dynamic_update_slice_in_dim(cells, mine, side * half, 0)
    return lax.dynamic_update_slice_in_dim(cells, came, (1 - side) * half, 0)


class Exchange:
    def __init__(self):
        self.outer = lax.axis_size("dp")
        self.inner = lax.axis_size("seq")
        outer_bits = [("dp", bit) for bit in bits_of(self.outer)]
        inner_bits = [("seq", bit) for bit in bits_of(self.inner)]
        rest = outer_bits[1:] + inner_bits[:-1]
        turn = len(outer_bits) - 1
        first = outer_bits[:1]
        last = inner_bits[-1:]
        self.orders = (first + rest + last, first + rest[turn:] + rest[:turn] + last)
        self.steps = len(self.orders[0])
        self.at = {"dp": lax.axis_index("dp"), "seq": lax.axis_index("seq")}

    def partner(self, flat, step):
        outer, inner = divmod(flat, self.inner)
        axis, bit = self.orders[outer & 1][step]
        if axis == "dp":
            outer ^= bit
        else:
            inner ^= bit
        return outer * self.inner + inner

    def swap(self, cells, step):
        devices = self.outer * self.inner
        pairs = [(flat, self.partner(flat, step)) for flat in range(devices)]
        return lax.ppermute(cells, ("dp", "seq"), pairs)

    def side(self, step):
        picked = [
            ((self.at[axis] & bit) != 0).astype(jnp.int32)
            for axis, bit in (order[step] for order in self.orders)
        ]
        return jnp.where((self.at["dp"] & 1) == 0, picked[0], picked[1])

    def scatter_sum(self, sent, kept, extra=None):
        for step in range(self.steps):
            if step > 0:
                half = cells.shape[0] // 2
                side = self.side(step)
                sent = lax.dynamic_slice_in_dim(cells, (1 - side) * half, half, 0).astype(BF16)
                kept = lax.dynamic_slice_in_dim(cells, side * half, half, 0)
            half = kept.shape[0]
            if extra is not None:
                high, low = split_two_outside(extra)
                sent = jnp.concatenate([sent, high, low], 0)
            came = self.swap(sent, step)
            cells = kept.astype(F32) + came[:half].astype(F32)
            if extra is not None:
                rows = extra.shape[0]
                mine = high.astype(F32) + low.astype(F32)
                extra = mine + (
                    came[half : half + rows].astype(F32) + came[half + rows :].astype(F32)
                )
        return cells.astype(BF16), extra

    def gather(self, cells):
        for step in reversed(range(self.steps)):
            cells = joined(cells, self.swap(cells, step), self.side(step))
        return cells


def local(
    byte_ids,
    item_lengths,
    block_counts,
    byte_embed,
    norm1_gain,
    norm1_shift,
    qkv_weight,
    out_weight,
    norm2_gain,
    norm2_shift,
    up_weight,
    up_bias,
    down_weight,
    down_bias,
    frontier_weight,
    pooled_cot,
):
    items, span = byte_ids.shape
    vocab, model_width = byte_embed.shape
    hidden_width = up_weight.shape[1]
    seq_count = lax.axis_size("seq")
    seq_place = lax.axis_index("seq")
    tokens = items * span
    wide = span + 2 * WIN
    tiles = span // TILE

    ends = range(seq_count - 1)
    ids_wide = jnp.concatenate(
        [
            lax.ppermute(byte_ids[:, span - WIN :], "seq", [(at, at + 1) for at in ends]),
            byte_ids,
            lax.ppermute(byte_ids[:, :WIN], "seq", [(at + 1, at) for at in ends]),
        ],
        1,
    )
    ids_row = ids_wide[:, None, :]
    ids_own = byte_ids[:, None, :]

    normed_one, table, key_table, value_table, cot_stack = call(
        table_kernel,
        1,
        [whole((vocab, model_width)), whole((1, model_width)), whole((1, model_width)),
         whole((model_width, 3 * model_width)), whole((items, NB, model_width)),
         whole((1, model_width))],
        [
            total_out((vocab, model_width), BF16),
            total_out((vocab, 3 * model_width), BF16),
            total_out((model_width, vocab), BF16),
            total_out((model_width, vocab), BF16),
            total_out((items, 3 * STACK, model_width), BF16),
        ],
        [],
        6 * vocab * model_width * model_width,
        (byte_embed, norm1_gain[None], norm1_shift[None], qkv_weight, pooled_cot,
         frontier_weight[None]),
    )

    first = (seq_place == 0).astype(jnp.int32)
    last = (seq_place == seq_count - 1).astype(jnp.int32)
    core = lax.axis_index("dp") & 1
    place = jnp.stack([seq_place * span, first, last, core]).astype(jnp.int32)

    square = (span, model_width)
    full = (span, hidden_width)
    row = (1, span)
    blocks = (NB, span)
    (
        attended, logs, middle, normed_two, act, slope, hidden_high, hidden_low,
        inner, frontier, running,
    ) = call(
        forward_kernel,
        items,
        [scalars(), scalars(), per_item((1, wide))]
        + [
            whole(shape)
            for shape in (
                (vocab, 3 * model_width), (model_width, vocab), (vocab, model_width),
                (model_width, model_width), (1, model_width), (1, model_width),
                (model_width, hidden_width), (1, hidden_width),
                (hidden_width, model_width), (1, model_width),
            )
        ]
        + [per_item((3 * STACK, model_width))],
        [
            item_out(items, square, BF16),
            item_out(items, (tiles * H // 2, 2 * TILE), F32),
            item_out(items, square, F32),
            item_out(items, square, BF16),
            item_out(items, full, BF16),
            item_out(items, full, BF16),
            item_out(items, square, BF16),
            item_out(items, square, BF16),
            item_out(items, blocks, F32),
            item_out(items, row, F32),
            item_out(items, row, F32),
        ],
        [
            pltpu.VMEM((3, SPAN_KEYS, 2 * TILE), F32),
            pltpu.VMEM((wide, 2 * model_width), BF16),
            pltpu.VMEM((model_width, wide), BF16),
            pltpu.VMEM((span, span), BF16),
        ],
        2 * tokens * model_width * (2 * hidden_width + 3 * model_width),
        (
            place, item_lengths, ids_row, table, value_table, byte_embed, out_weight,
            norm2_gain[None], norm2_shift[None], up_weight, up_bias[None], down_weight,
            down_bias[None], cot_stack,
        ),
    )

    mass_before, item_total, _, _ = scan_over("seq", running[:, 0, span - 1], seq_place)
    numbers = (place, item_lengths, block_counts, mass_before, item_total, running)
    numbers_specs = [scalars()] * 5 + [per_item(row)]

    (stats,) = call(
        stats_kernel,
        items,
        numbers_specs + [per_item(blocks)],
        [item_out(items, (8, NB), F32)],
        [],
        tokens * NB,
        numbers + (inner,),
    )
    (numer,) = call(
        numer_kernel,
        items,
        numbers_specs + [per_item(square), per_item(square)],
        [item_out(items, (NB, model_width), F32)],
        [],
        6 * tokens * NB * model_width,
        numbers + (hidden_high, hidden_low),
    )
    _, stats_whole, stats_after, numer = scan_over("seq", stats, seq_place, numer)

    back_specs = numbers_specs + [
        per_item(row), per_item(blocks), per_item((8, NB)), per_item((8, NB)),
        per_item((3 * STACK, model_width)),
    ]
    (
        down_sent, down_kept, up_sent, up_kept, d_attended, d_embed_direct, rows,
    ) = call(
        back_kernel,
        items,
        back_specs
        + [per_item(row), per_item(full), per_item(full)]
        + [per_item(square)] * 5
        + [whole((1, model_width)), whole((hidden_width, model_width)),
           whole((model_width, hidden_width)), whole((model_width, model_width))],
        halves_out(hidden_width, model_width)
        + halves_out(hidden_width + model_width, model_width)
        + [
            item_out(items, square, BF16),
            total_out((vocab, model_width)),
            total_out((8, model_width)),
        ],
        [
            pltpu.VMEM((span, span), BF16),
            pltpu.VMEM((hidden_width, model_width), F32),
            pltpu.VMEM((hidden_width + model_width, model_width), F32),
        ],
        6 * tokens * hidden_width * model_width,
        numbers
        + (frontier, inner, stats_whole, stats_after, cot_stack, ids_own, act, slope,
           hidden_high, hidden_low, middle, normed_two, attended, norm2_gain[None],
           down_weight, up_weight, out_weight),
    )

    exchange = Exchange()
    rows_sent, rows_kept = call(
        attend_back_kernel,
        items,
        [scalars(), per_item((1, wide)), whole((vocab, 3 * model_width)),
         whole((model_width, vocab)), per_item(square), per_item((tiles * H // 2, 2 * TILE)),
         whole((vocab, model_width))],
        halves_out(4 * vocab, model_width),
        [
            pltpu.VMEM((4 * vocab, model_width), F32),
            pltpu.VMEM((3, SPAN_KEYS, 2 * TILE), F32),
            pltpu.VMEM((wide, 3 * model_width), BF16),
            pltpu.VMEM((model_width, wide), BF16),
            pltpu.VMEM((model_width, span), BF16),
            pltpu.VMEM((wide, model_width), F32),
            pltpu.VMEM((wide, model_width), F32),
            pltpu.VMEM((model_width, vocab), F32),
        ],
        10 * tokens * SPAN_KEYS * model_width,
        (place, ids_row, table, key_table, d_attended, logs, d_embed_direct),
    )

    inverse = 1.0 / (stats_whole[:, 0] + 1.0)
    pooled = all_sum("seq", numer.reshape(items * NB, model_width)).reshape(
        items, NB, model_width
    ) * inverse[:, :, None]

    devices = exchange.outer * exchange.inner
    down_share, _ = exchange.scatter_sum(down_sent, down_kept)
    weights_share, rows = exchange.scatter_sum(up_sent, up_kept, rows)
    small_share, _ = exchange.scatter_sum(rows_sent, rows_kept)
    cut = down_share.shape[0]
    big = exchange.gather(jnp.concatenate([down_share, weights_share], 0))
    big = big.reshape(devices, -1, model_width)
    d_down = big[:, :cut].reshape(hidden_width, model_width).astype(F32)
    d_weights = big[:, cut:].reshape(-1, model_width).astype(F32)
    small = exchange.gather(small_share)

    d_up = jnp.concatenate(
        [
            d_weights[begin : begin + model_width]
            for begin in range(0, hidden_width, model_width)
        ],
        1,
    )
    d_out = d_weights[hidden_width:]
    d_table = jnp.concatenate(
        [small[at * vocab : (at + 1) * vocab] for at in range(1, 4)], 1
    )
    d_qkv = dot_first(normed_one, d_table)
    d_normed_one = dot_last(d_table, qkv_weight)
    embed_rows = byte_embed.astype(F32)
    centered = embed_rows - jnp.mean(embed_rows, -1, keepdims=True)
    scale_one = lax.rsqrt(jnp.mean(centered * centered, -1, keepdims=True) + eps)
    unit_one = centered * scale_one
    d_gain_one = jnp.sum(d_normed_one * unit_one, 0)
    d_shift_one = jnp.sum(d_normed_one, 0)
    pushed = d_normed_one * norm1_gain
    d_embed = small[:vocab].astype(F32) + scale_one * (
        pushed
        - jnp.mean(pushed, -1, keepdims=True)
        - unit_one * jnp.mean(pushed * unit_one, -1, keepdims=True)
    )
    return (
        pooled,
        d_embed,
        d_gain_one,
        d_shift_one,
        d_qkv,
        d_out,
        rows[0],
        rows[1],
        d_up,
        rows[4:].reshape(-1),
        d_down,
        rows[2],
        rows[3],
    )


def solution(mesh):
    placed = (P("dp", "seq"), P("dp"), P("dp")) + (P(),) * 12 + (P("dp", None, None),)
    return jax.shard_map(
        local,
        mesh=mesh,
        in_specs=placed,
        out_specs=(P("dp", None, None),) + (P(),) * 12,
        check_vma=False,
    )
```

```python
import functools

import jax
import jax.numpy as jnp
from jax import lax
from jax.experimental import pallas as pl
from jax.experimental.pallas import tpu as pltpu
from jax.sharding import PartitionSpec as P

H = 8
HD = 64
WIN = 64
NB = 64
TILE = 128
SPAN_KEYS = TILE + 2 * WIN
PAIR = 2 * HD
STACK = 80

eps = 1e-05
spread = 2.0
LOG2E = 1.4426950408889634
F32 = jnp.float32
BF16 = jnp.bfloat16
VMEM_BYTES = 56 * 1024 * 1024


def dot(left, right):
    return jnp.dot(left, right, preferred_element_type=F32)


def dot_last(left, right):
    return lax.dot_general(left, right, (((1,), (1,)), ((), ())), preferred_element_type=F32)


def dot_first(left, right):
    return lax.dot_general(left, right, (((0,), (0,)), ((), ())), preferred_element_type=F32)


def split_two_outside(value):
    high = lax.reduce_precision(value, 8, 7)
    return high.astype(BF16), (value - high).astype(BF16)


def split_two(value):
    high = value.astype(BF16)
    return high, (value - high.astype(F32)).astype(BF16)


def iota(shape, dim):
    return lax.broadcasted_iota(jnp.int32, shape, dim)


def one_hot_columns(ids_row, vocab):
    cells = iota((vocab, ids_row.shape[1]), 0)
    return jnp.where(cells == ids_row, 1.0, 0.0).astype(BF16)


def gelu_with_slope(value):
    below = 0.5 + 0.5 * lax.erf(value * 0.7071067811865476)
    bell = jnp.exp2(value * value * (-0.5 * LOG2E))
    return value * below, below + value * (bell * 0.3989422804014327)


def window_bias(first, last):
    key_at = iota((SPAN_KEYS, 2 * TILE), 0)
    query_at = iota((SPAN_KEYS, 2 * TILE), 1) & (TILE - 1)
    reach = key_at - query_at
    seen = (reach >= 0) & (reach <= 2 * WIN)
    seen_first = seen & (key_at >= WIN * first)
    seen_last = seen & (key_at < SPAN_KEYS - WIN * last)
    return [jnp.where(kept, 0.0, -1e30) for kept in (seen_first, seen, seen_last)]


def head_blocks(pair_rows):
    lane = iota(pair_rows.shape, 1)
    blank = jnp.zeros_like(pair_rows)
    return jnp.concatenate(
        [jnp.where(lane < HD, pair_rows, blank), jnp.where(lane < HD, blank, pair_rows)], 0
    )


def head_columns(pair_columns):
    return jnp.concatenate([pair_columns[:HD, :TILE], pair_columns[HD:, TILE:]], 0)


def running_sum(row, ones_matrix):
    one, rest = split_two(row)
    high = one.astype(F32) + rest.astype(F32)
    two = (row - high).astype(BF16)
    width = row.shape[1]
    parts = jnp.concatenate([one, rest, two, jnp.zeros((13, width), BF16)], 0)
    sums = dot(parts, ones_matrix)
    return sums[0:1] + sums[1:2] + sums[2:3]


def table_kernel(
    embed, gain, shift, weight, cot, frontier_weight,
    normed_out, table_out, key_out, value_out, stack_out,
):
    rows = embed[...].astype(F32)
    centered = rows - jnp.mean(rows, -1, keepdims=True)
    scale = lax.rsqrt(jnp.mean(centered * centered, -1, keepdims=True) + eps)
    normed = (centered * scale * gain[...] + shift[...]).astype(BF16)
    normed_out[...] = normed
    model_width = rows.shape[1]
    table = dot(normed, weight[...])
    queries = table[:, :model_width].astype(BF16).astype(F32) * HD**-0.5
    table_out[:, :model_width] = queries.astype(BF16)
    table_out[:, model_width:] = table[:, model_width:].astype(BF16)
    key_out[...] = table[:, model_width : 2 * model_width].T.astype(BF16)
    value_out[...] = table[:, 2 * model_width :].T.astype(BF16)
    rim_high, rim_low = split_two(
        jnp.where(iota((STACK - NB, model_width), 0) == 0, frontier_weight[...], 0.0)
    )
    for item in range(cot.shape[0]):
        high, low = split_two(cot[item])
        for at, (block, rim) in enumerate(((high, rim_high), (high, rim_high), (low, rim_low))):
            stack_out[item, at * STACK : at * STACK + NB] = block
            stack_out[item, at * STACK + NB : (at + 1) * STACK] = rim


def take_turns(*parts):
    parts = list(parts)
    while parts:
        for part in list(parts):
            if next(part, None) is None:
                parts.remove(part)


def forward_kernel(
    place, lengths, ids_row, table, value_table, embed, out_weight, gain, shift,
    up_weight, up_bias, down_weight, down_bias, cot_stack,
    attended_out, log_out, middle_out, normed_out, act_out, slope_out, high_out, low_out,
    inner_out, frontier_out, running_out,
    bias, query_keys, value_columns, triangle, held_hot, held_attended,
):
    step = pl.program_id(0)
    items = pl.num_programs(0) - 1
    span = middle_out.shape[1]
    model_width = middle_out.shape[2]
    vocab = embed.shape[0]
    hidden_width = up_weight.shape[1]

    @pl.when(step == 0)
    def _():
        for at, tile in enumerate(window_bias(place[1], place[2])):
            bias[at] = tile
        triangle[...] = jnp.where(
            iota((span, span), 0) <= iota((span, span), 1), 1.0, 0.0
        ).astype(BF16)

    def attend():
        hot_columns = one_hot_columns(ids_row[0], vocab)
        hot = hot_columns.T
        query_keys[...] = dot(hot, table[:, : 2 * model_width]).astype(BF16)
        value_columns[...] = dot(value_table[...], hot_columns).astype(BF16)
        held_hot[...] = hot[WIN : WIN + span]
        yield True
        tiles = span // TILE
        pairs = H // 2
        for tile in range(tiles):
            begin = tile * TILE
            window = slice(begin, begin + SPAN_KEYS)
            tile_bias = bias[0 if tile == 0 else (2 if tile == tiles - 1 else 1)]
            lanes = [slice(pair * PAIR, (pair + 1) * PAIR) for pair in range(pairs)]
            scores = []
            for pair in range(pairs):
                key_lanes = slice(model_width + pair * PAIR, model_width + (pair + 1) * PAIR)
                query_block = head_blocks(query_keys[begin + WIN : begin + WIN + TILE, lanes[pair]])
                scores.append(dot_last(query_keys[window, key_lanes], query_block) + tile_bias)
            yield True
            probs = []
            for pair in range(pairs):
                peak = jnp.max(scores[pair], 0, keepdims=True)
                weights = jnp.exp(scores[pair] - peak)
                weight_sum = jnp.sum(weights, 0, keepdims=True)
                probs.append((weights * pltpu.reciprocal(weight_sum, approx=True)).astype(BF16))
                at = tile * pairs + pair
                log_out[0, at : at + 1, :] = peak + jnp.log(weight_sum)
            yield True
            mixed = [dot(value_columns[lanes[pair], window], probs[pair]) for pair in range(pairs)]
            for pair in range(pairs):
                rows = head_columns(mixed[pair]).T.astype(BF16)
                attended_out[0, begin : begin + TILE, lanes[pair]] = rows
                held_attended[begin : begin + TILE, lanes[pair]] = rows
            yield True

    def feed():
        middle = dot(held_hot[...], embed[...]) + dot(held_attended[...], out_weight[...])
        middle_out[0] = middle
        centered = middle - jnp.mean(middle, -1, keepdims=True)
        variance = jnp.mean(centered * centered, -1, keepdims=True)
        normed = (centered * lax.rsqrt(variance + eps) * gain[...] + shift[...]).astype(BF16)
        normed_out[0] = normed
        yield True
        chunk = 512
        cuts = [slice(begin, begin + chunk) for begin in range(0, hidden_width, chunk)]
        hidden = middle + down_bias[...]
        preact = dot(normed, up_weight[:, cuts[0]]) + up_bias[:, cuts[0]]
        for at, cells in enumerate(cuts):
            held = preact
            if at + 1 < len(cuts):
                preact = dot(normed, up_weight[:, cuts[at + 1]]) + up_bias[:, cuts[at + 1]]
            yield True
            act, slope = gelu_with_slope(held)
            act = act.astype(BF16)
            act_out[0, :, cells] = act
            slope_out[0, :, cells] = slope.astype(BF16)
            yield True
            hidden = hidden + dot(act, down_weight[cells, :])
            yield True
        high, low = split_two(hidden)
        high_out[0] = high
        low_out[0] = low
        products = dot_last(cot_stack[0, STACK:, :], high)
        inner = products[:STACK] + products[STACK:] + dot_last(cot_stack[0, :STACK, :], low)
        inner_out[0] = inner[:NB]
        frontier = 1.0 / (1.0 + jnp.exp(-inner[NB : NB + 1]))
        frontier_out[0] = frontier
        slot = place[0] + iota((1, span), 1)
        running_out[0] = running_sum(
            jnp.where(slot < lengths[step - 1], frontier, 0.0), triangle[...]
        )
        yield True

    @pl.when(step == 0)
    def _():
        take_turns(attend())

    @pl.when((step > 0) & (step < items))
    def _():
        take_turns(feed(), attend())

    @pl.when(step == items)
    def _():
        take_turns(feed())


def assignment(place, lengths, counts, before, total, running):
    item = pl.program_id(0)
    span = running.shape[2]
    slot = place[0] + iota((1, span), 1)
    inside = slot < lengths[item]
    count = counts[item].astype(F32)
    position = count * (running[0] + before[item]) / total[item]
    block_at = iota((NB, span), 0)
    distance = position - (block_at.astype(F32) + 0.5)
    kept = inside & (block_at < counts[item])
    assign = jnp.where(kept, jnp.exp(-spread * distance * distance), 0.0)
    return position, assign, assign * distance * (-2.0 * spread), inside, count


def stats_kernel(place, lengths, counts, before, total, running, inner, stats_out):
    position, assign, pull, _, _ = assignment(place, lengths, counts, before, total, running)
    pull_inner = pull * inner[0]
    lane = iota((NB, 128), 1)
    stats = jnp.zeros((NB, 128), F32)
    terms = (
        assign, assign * inner[0], pull, pull_inner, pull * position, pull_inner * position,
    )
    for at, cells in enumerate(terms):
        stats = jnp.where(lane == at, jnp.sum(cells, 1, keepdims=True), stats)
    stats_out[0] = stats.T[:8]


def numer_kernel(place, lengths, counts, before, total, running, high, low, numer_out):
    _, assign, _, _, _ = assignment(place, lengths, counts, before, total, running)
    assign_high, assign_low = split_two(assign)
    numer_out[0] = (
        dot(assign_high, high[0]) + dot(assign_low, high[0]) + dot(assign_high, low[0])
    )


def hidden_gradient(
    place, lengths, counts, before, total, running, frontier, inner, whole_stats, after_stats,
    triangle,
):
    item = pl.program_id(0)
    span = running.shape[2]
    position, assign, pull, inside, count = assignment(
        place, lengths, counts, before, total, running
    )
    whole_columns = whole_stats[0].T
    after_columns = after_stats[0].T
    inverse = 1.0 / (whole_columns[:, 0:1] + 1.0)
    d_denom = -inverse * inverse * whole_columns[:, 1:2]
    push = jnp.sum(
        d_denom * after_columns[:, 2:3] + inverse * after_columns[:, 3:4], 0, keepdims=True
    )
    pushed = jnp.sum(
        d_denom * whole_columns[:, 4:5] + inverse * whole_columns[:, 5:6], 0, keepdims=True
    )
    d_position = jnp.sum((inner[0] * inverse + d_denom) * pull, 0, keepdims=True)
    d_cumulative = d_position * count / total[item]
    d_prob = running_sum(d_cumulative, triangle[...]) + (push * count - pushed) / total[item]
    share = frontier[0]
    d_logit = jnp.where(inside, d_prob * share * (1.0 - share), 0.0)
    left = jnp.concatenate(
        [assign * inverse, d_logit, jnp.zeros((STACK - NB - 1, span), F32)], 0
    )
    return split_two(left)


def write_halves(place, total, sent_out, kept_out):
    half = kept_out.shape[0]
    core = place[3]
    sent_out[:half] = total[pl.ds(pl.multiple_of((1 - core) * half, half), half)].astype(BF16)
    kept_out[...] = total[pl.ds(pl.multiple_of(core * half, half), half)].astype(BF16)


def suffix_ones(triangle):
    triangle[...] = jnp.where(
        iota(triangle.shape, 0) >= iota(triangle.shape, 1), 1.0, 0.0
    ).astype(BF16)


def back_kernel(
    place, lengths, counts, before, total, running, frontier, inner, whole_stats, after_stats,
    cot_stack, ids_row, act, slope, high, low, middle, normed, attended, gain, down_weight,
    up_weight, out_weight,
    down_sent, down_kept, up_sent, up_kept, attended_out, embed_out, rows_out,
    triangle, down_total, up_total,
):
    hidden_width = up_weight.shape[1]
    model_width = up_weight.shape[0]
    vocab = embed_out.shape[0]

    @pl.when(pl.program_id(0) == 0)
    def _():
        suffix_ones(triangle)
        for cells in (down_total, up_total, embed_out, rows_out):
            cells[...] = jnp.zeros_like(cells)

    left_high, left_low = hidden_gradient(
        place, lengths, counts, before, total, running, frontier, inner, whole_stats,
        after_stats, triangle,
    )
    d_hidden = dot_first(jnp.concatenate([left_high, left_low, left_high], 0), cot_stack[0])
    d_low = d_hidden.astype(BF16)
    cuts = [
        slice(begin, begin + model_width) for begin in range(0, hidden_width, model_width)
    ]
    d_act = dot_last(d_low, down_weight[cuts[0], :])
    d_normed = None
    for at, cells in enumerate(cuts):
        held = d_act
        if at + 1 < len(cuts):
            d_act = dot_last(d_low, down_weight[cuts[at + 1], :])
        d_preact = (held * slope[0, :, cells].astype(F32)).astype(BF16)
        down_total[cells, :] += dot_first(act[0, :, cells], d_low)
        part = dot_last(d_preact, up_weight[:, cells])
        d_normed = part if d_normed is None else d_normed + part
        up_total[cells, :] += dot_first(normed[0], d_preact)
        rows_out[4 + at : 5 + at] += jnp.sum(d_preact.astype(F32), 0, keepdims=True)
    rows = middle[0]
    centered = rows - jnp.mean(rows, -1, keepdims=True)
    scale = lax.rsqrt(jnp.mean(centered * centered, -1, keepdims=True) + eps)
    unit = centered * scale
    tail = slice(NB, STACK)
    products = (
        dot(left_high[tail], high[0]) + dot(left_low[tail], high[0]) + dot(left_high[tail], low[0])
    )
    rows_out[2:3] += jnp.sum(d_low.astype(F32), 0, keepdims=True)
    rows_out[3:4] += products[0:1]
    rows_out[0:1] += jnp.sum(d_normed * unit, 0, keepdims=True)
    rows_out[1:2] += jnp.sum(d_normed, 0, keepdims=True)
    pushed = d_normed * gain[...]
    d_middle = d_hidden + scale * (
        pushed
        - jnp.mean(pushed, -1, keepdims=True)
        - unit * jnp.mean(pushed * unit, -1, keepdims=True)
    )
    middle_high, middle_low = split_two(d_middle)
    attended_out[0] = dot_last(middle_high, out_weight[...]).astype(BF16)
    up_total[hidden_width:, :] += dot_first(attended[0], middle_high)
    hot = one_hot_columns(ids_row[0], vocab)
    embed_out[...] += dot(hot, middle_high) + dot(hot, middle_low)

    @pl.when(pl.program_id(0) == pl.num_programs(0) - 1)
    def _():
        write_halves(place, down_total, down_sent, down_kept)
        write_halves(place, up_total, up_sent, up_kept)
        rows = up_kept.shape[0]
        high, low = split_two(rows_out[...])
        up_sent[rows:] = jnp.concatenate([high, low], 0)


def attend_back_kernel(
    place, ids_row, table, key_table, d_attended, logs, rows_in,
    *outs_and_scratch,
):
    *outs, rows_total, bias, table_rows, key_columns, d_queries, d_keys, d_values, (
        queries_total
    ) = outs_and_scratch
    item = pl.program_id(0)
    span = d_attended.shape[1]
    model_width = d_attended.shape[2]
    vocab = table.shape[0]

    @pl.when(item == 0)
    def _():
        for at, tile in enumerate(window_bias(place[1], place[2])):
            bias[at] = tile
        given = rows_in.shape[0]
        rows_total[:given] = rows_in[...]
        if given < 4 * vocab:
            rows_total[given:] = jnp.zeros((4 * vocab - given, model_width), F32)
        queries_total[...] = jnp.zeros_like(queries_total)

    hot_columns = one_hot_columns(ids_row[0], vocab)
    hot = hot_columns.T
    table_rows[...] = dot(hot, table[...]).astype(BF16)
    key_columns[...] = dot(key_table[...], hot_columns).astype(BF16)
    d_keys[...] = jnp.zeros_like(d_keys)
    d_values[...] = jnp.zeros_like(d_values)
    tiles = span // TILE
    pairs = H // 2
    for tile in range(tiles):
        begin = tile * TILE
        tile_bias = bias[0 if tile == 0 else (2 if tile == tiles - 1 else 1)]
        window = slice(begin, begin + SPAN_KEYS)
        lanes = [slice(pair * PAIR, (pair + 1) * PAIR) for pair in range(pairs)]
        query_blocks, grad_blocks, scores, d_probs = [], [], [], []
        for pair in range(pairs):
            key_lanes = slice(model_width + pair * PAIR, model_width + (pair + 1) * PAIR)
            value_lanes = slice(2 * model_width + pair * PAIR, 2 * model_width + (pair + 1) * PAIR)
            query_blocks.append(
                head_blocks(table_rows[begin + WIN : begin + WIN + TILE, lanes[pair]])
            )
            grad_blocks.append(head_blocks(d_attended[0, begin : begin + TILE, lanes[pair]]))
            scores.append(dot_last(table_rows[window, key_lanes], query_blocks[pair]) + tile_bias)
            d_probs.append(dot_last(table_rows[window, value_lanes], grad_blocks[pair]))
        probs_low, d_scores = [], []
        for pair in range(pairs):
            at = tile * pairs + pair
            probs = jnp.exp(scores[pair] - logs[0, at : at + 1, :])
            weighted = probs * d_probs[pair]
            probs_low.append(probs.astype(BF16))
            d_scores.append(
                (weighted - probs * jnp.sum(weighted, 0, keepdims=True)).astype(BF16)
            )
        for pair in range(pairs):
            d_values[window, lanes[pair]] += dot(probs_low[pair], grad_blocks[pair])
            d_keys[window, lanes[pair]] += dot(d_scores[pair], query_blocks[pair])
        turned = [dot(key_columns[lanes[pair], window], d_scores[pair]) for pair in range(pairs)]
        for pair in range(pairs):
            d_queries[lanes[pair], begin : begin + TILE] = (
                head_columns(turned[pair]) * (HD**-0.5)
            ).astype(BF16)
    queries_total[...] += dot(d_queries[...], hot[WIN : WIN + span])
    rows_total[2 * vocab : 3 * vocab] += dot(hot_columns, d_keys[...].astype(BF16))
    rows_total[3 * vocab :] += dot(hot_columns, d_values[...].astype(BF16))

    @pl.when(item == pl.num_programs(0) - 1)
    def _():
        rows_total[vocab : 2 * vocab] += queries_total[...].T
        if len(outs) == 2:
            write_halves(place, rows_total, *outs)
        else:
            outs[0][...] = rows_total[...]


def finish_kernel(
    embed, normed, gain, weight, sums,
    embed_out, weight_out, gain_out, shift_out,
):
    vocab, model_width = embed.shape
    rows = embed[...].astype(F32)
    centered = rows - jnp.mean(rows, -1, keepdims=True)
    scale = lax.rsqrt(jnp.mean(centered * centered, -1, keepdims=True) + eps)
    unit = centered * scale
    d_normed = None
    for at in range(3):
        lanes = slice(at * model_width, (at + 1) * model_width)
        part = sums[(at + 1) * vocab : (at + 2) * vocab]
        weight_out[:, lanes] = dot_first(normed[...], part)
        back = dot_last(part, weight[:, lanes])
        d_normed = back if d_normed is None else d_normed + back
    gain_out[...] = jnp.sum(d_normed * unit, 0, keepdims=True)
    shift_out[...] = jnp.sum(d_normed, 0, keepdims=True)
    pushed = d_normed * gain[...]
    embed_out[...] = sums[:vocab].astype(F32) + scale * (
        pushed
        - jnp.mean(pushed, -1, keepdims=True)
        - unit * jnp.mean(pushed * unit, -1, keepdims=True)
    )


def whole(shape):
    return pl.BlockSpec(shape, lambda item: (0,) * len(shape))


def per_item(shape):
    return pl.BlockSpec((1,) + shape, lambda item: (item,) + (0,) * len(shape))


def item_from(shape, first):
    return pl.BlockSpec((1,) + shape, lambda item: (item + first,) + (0,) * len(shape))


def scalars():
    return pl.BlockSpec(memory_space=pltpu.SMEM)


def call(kernel, items, in_specs, outs, scratch, flops, arrays):
    flops = 1
    shapes = [jax.ShapeDtypeStruct(shape, dtype) for _, shape, dtype in outs]
    return pl.pallas_call(
        kernel,
        grid=(items,),
        in_specs=in_specs,
        out_specs=[spec for spec, _, _ in outs],
        out_shape=shapes,
        scratch_shapes=scratch,
        compiler_params=pltpu.CompilerParams(vmem_limit_bytes=VMEM_BYTES),
        cost_estimate=pl.CostEstimate(flops=flops, bytes_accessed=0, transcendentals=0),
    )(*arrays)


def item_out(items, shape, dtype):
    return per_item(shape), (items,) + shape, dtype


def halves_out(rows, width, more=0):
    return [total_out((rows // 2 + more, width), BF16), total_out((rows // 2, width), BF16)]


def total_out(shape, dtype=F32):
    return whole(shape), shape, dtype


def bits_of(count):
    return [1 << at for at in range(count.bit_length() - 1)]


def scan_over(axis, cells, index, beside=None):
    count = lax.axis_size(axis)
    earlier = jnp.zeros_like(cells)
    later = jnp.zeros_like(cells)
    for step, bit in enumerate(bits_of(count)):
        if step == 1 and beside is not None:
            cells, beside = lax.optimization_barrier((cells, beside))
        other = lax.ppermute(cells, axis, [(at, at ^ bit) for at in range(count)])
        upper = (index & bit) != 0
        earlier = earlier + jnp.where(upper, other, 0.0)
        later = later + jnp.where(upper, 0.0, other)
        cells = cells + other
    return earlier, cells, later, beside


def joined(mine, came, side):
    half = mine.shape[0]
    cells = jnp.zeros((2 * half,) + mine.shape[1:], mine.dtype)
    cells = lax.dynamic_update_slice_in_dim(cells, mine, side * half, 0)
    return lax.dynamic_update_slice_in_dim(cells, came, (1 - side) * half, 0)


class Exchange:
    def __init__(self, outer_first):
        outer_bits = [("dp", bit) for bit in bits_of(lax.axis_size("dp"))]
        inner_bits = [("seq", bit) for bit in bits_of(lax.axis_size("seq"))]
        core, last = outer_bits[:1], inner_bits[-1:]
        outer_bits, inner_bits = outer_bits[1:], inner_bits[:-1]
        if outer_first:
            cut = len(outer_bits)
            near, far = inner_bits[:cut], inner_bits[cut:]
            self.orders = (
                core + outer_bits + near + far + last,
                core + near + outer_bits + far + last,
            )
        else:
            self.orders = (
                core + inner_bits + outer_bits + last,
                core + inner_bits[::-1] + outer_bits + last,
            )
        self.steps = len(self.orders[0])

    def swap(self, cells, step):
        outer_size, inner_size = lax.axis_size("dp"), lax.axis_size("seq")
        pairs = []
        for flat in range(outer_size * inner_size):
            outer, inner = divmod(flat, inner_size)
            axis, bit = self.orders[outer & 1][step]
            other = (outer ^ bit, inner) if axis == "dp" else (outer, inner ^ bit)
            pairs.append((flat, other[0] * inner_size + other[1]))
        return lax.ppermute(cells, ("dp", "seq"), pairs)

    def side(self, step):
        sides = [
            ((lax.axis_index(axis) & bit) != 0).astype(jnp.int32)
            for axis, bit in (order[step] for order in self.orders)
        ]
        return jnp.where((lax.axis_index("dp") & 1) == 0, sides[0], sides[1])

    def shared(self, step):
        axis, _ = self.orders[0][step]
        return axis == "seq" and self.orders[0][step] == self.orders[1][step]


def halves(cells, side):
    half = cells.shape[0] // 2
    return (
        lax.dynamic_slice_in_dim(cells, (1 - side) * half, half, 0),
        lax.dynamic_slice_in_dim(cells, side * half, half, 0),
    )


class Chain:
    def __init__(self, exchange, sent, kept, vectors=None, stop=None):
        self.exchange = exchange
        self.sent = sent
        self.kept = kept
        self.cells = None
        self.vectors = vectors
        self.rider = None
        self.stop = exchange.steps if stop is None else stop
        gathers = range(self.stop - 1, -1, -1)
        self.plan = [("sum", step) for step in range(exchange.steps)]
        self.plan += [("gather", step) for step in gathers]
        self.at = 0
        self.came = None

    def start(self):
        kind, step = self.plan[self.at]
        if kind == "gather" or step >= self.stop:
            moved = [self.cells]
        else:
            moved = [self.sent]
            if self.vectors is not None and step > 0:
                moved += split_two_outside(self.vectors)
        if self.rider is not None and self.exchange.shared(step):
            if kind == "sum":
                away, self.rider = halves(self.rider, self.exchange.side(step))
                moved.append(away.astype(BF16))
            else:
                moved.append(self.rider.astype(BF16))
        moved = moved[0] if len(moved) == 1 else jnp.concatenate(moved, 0)
        self.came = self.exchange.swap(moved, step)

    def finish(self):
        kind, step = self.plan[self.at]
        came, self.came = self.came, None
        self.at += 1
        side = self.exchange.side(step)
        if kind == "gather":
            rows = self.cells.shape[0]
            if self.rider is not None and self.exchange.shared(step):
                self.rider = joined(self.rider.astype(BF16), came[rows:], side)
            self.cells = joined(self.cells, came[:rows], side)
            return
        if step >= self.stop:
            self.cells = (self.cells.astype(F32) + came.astype(F32)).astype(BF16)
            return
        half = self.kept.shape[0]
        if self.vectors is not None:
            rows = self.vectors.shape[0]
            high, low = split_two_outside(self.vectors)
            self.vectors = (high.astype(F32) + low.astype(F32)) + (
                came[half : half + rows].astype(F32)
                + came[half + rows : half + 2 * rows].astype(F32)
            )
        if self.rider is not None and self.exchange.shared(step):
            self.rider = self.rider + came[half : half + self.rider.shape[0]].astype(F32)
        if step + 1 == self.stop:
            self.cells = (self.kept.astype(F32) + came[:half].astype(F32)).astype(BF16)
            return
        side = self.exchange.side(step + 1)
        away, stay = halves(self.kept, side)
        came_away, came_stay = halves(came[:half], side)
        self.sent = (away.astype(F32) + came_away.astype(F32)).astype(BF16)
        self.kept = stay.astype(F32) + came_stay.astype(F32)

    def run(self, until=None):
        until = len(self.plan) if until is None else until
        while self.at < until:
            if self.came is None:
                self.start()
            self.finish()


def local(
    byte_ids,
    item_lengths,
    block_counts,
    byte_embed,
    norm1_gain,
    norm1_shift,
    qkv_weight,
    out_weight,
    norm2_gain,
    norm2_shift,
    up_weight,
    up_bias,
    down_weight,
    down_bias,
    frontier_weight,
    pooled_cot,
):
    items, span = byte_ids.shape
    vocab, model_width = byte_embed.shape
    hidden_width = up_weight.shape[1]
    seq_count = lax.axis_size("seq")
    seq_place = lax.axis_index("seq")
    tokens = items * span
    wide = span + 2 * WIN
    tiles = span // TILE

    ends = range(seq_count - 1)
    ids_wide = jnp.concatenate(
        [
            lax.ppermute(byte_ids[:, span - WIN :], "seq", [(at, at + 1) for at in ends]),
            byte_ids,
            lax.ppermute(byte_ids[:, :WIN], "seq", [(at + 1, at) for at in ends]),
        ],
        1,
    )
    ids_row = ids_wide[:, None, :]
    ids_own = byte_ids[:, None, :]

    normed_one, table, key_table, value_table, cot_stack = call(
        table_kernel,
        1,
        [whole((vocab, model_width)), whole((1, model_width)), whole((1, model_width)),
         whole((model_width, 3 * model_width)), whole((items, NB, model_width)),
         whole((1, model_width))],
        [
            total_out((vocab, model_width), BF16),
            total_out((vocab, 3 * model_width), BF16),
            total_out((model_width, vocab), BF16),
            total_out((model_width, vocab), BF16),
            total_out((items, 3 * STACK, model_width), BF16),
        ],
        [],
        6 * vocab * model_width * model_width,
        (byte_embed, norm1_gain[None], norm1_shift[None], qkv_weight, pooled_cot,
         frontier_weight[None]),
    )

    first = (seq_place == 0).astype(jnp.int32)
    last = (seq_place == seq_count - 1).astype(jnp.int32)
    core = lax.axis_index("dp") & 1
    place = jnp.stack([seq_place * span, first, last, core]).astype(jnp.int32)

    square = (span, model_width)
    full = (span, hidden_width)
    row = (1, span)
    blocks = (NB, span)
    logs_shape = (tiles * H // 2, 2 * TILE)

    def item_ahead(shape):
        return pl.BlockSpec(
            (1,) + shape, lambda step: (jnp.minimum(step, items - 1),) + (0,) * len(shape)
        )

    def item_behind(shape):
        return pl.BlockSpec(
            (1,) + shape, lambda step: (jnp.maximum(step - 1, 0),) + (0,) * len(shape)
        )

    (
        attended, logs, middle, normed_two, act, slope, hidden_high, hidden_low,
        inner, frontier, running,
    ) = call(
        forward_kernel,
        items + 1,
        [scalars(), scalars(), item_ahead((1, wide))]
        + [
            whole(shape)
            for shape in (
                (vocab, 3 * model_width), (model_width, vocab), (vocab, model_width),
                (model_width, model_width), (1, model_width), (1, model_width),
                (model_width, hidden_width), (1, hidden_width),
                (hidden_width, model_width), (1, model_width),
            )
        ]
        + [item_behind((3 * STACK, model_width))],
        [
            (item_ahead(square), (items,) + square, BF16),
            (item_ahead(logs_shape), (items,) + logs_shape, F32),
        ]
        + [
            (item_behind(shape), (items,) + shape, dtype)
            for shape, dtype in (
                (square, F32), (square, BF16), (full, BF16), (full, BF16), (square, BF16),
                (square, BF16), (blocks, F32), (row, F32), (row, F32),
            )
        ],
        [
            pltpu.VMEM((3, SPAN_KEYS, 2 * TILE), F32),
            pltpu.VMEM((wide, 2 * model_width), BF16),
            pltpu.VMEM((model_width, wide), BF16),
            pltpu.VMEM((span, span), BF16),
            pltpu.VMEM((span, vocab), BF16),
            pltpu.VMEM(square, BF16),
        ],
        2 * tokens * model_width * (2 * hidden_width + 3 * model_width),
        (
            place, item_lengths, ids_row, table, value_table, byte_embed, out_weight,
            norm2_gain[None], norm2_shift[None], up_weight, up_bias[None], down_weight,
            down_bias[None], cot_stack,
        ),
    )

    mass_before, item_total, _, _ = scan_over("seq", running[:, 0, span - 1], seq_place)
    numbers = (place, item_lengths, block_counts, mass_before, item_total, running)
    numbers_specs = [scalars()] * 5 + [per_item(row)]

    (stats,) = call(
        stats_kernel,
        items,
        numbers_specs + [per_item(blocks)],
        [item_out(items, (8, NB), F32)],
        [],
        tokens * NB,
        numbers + (inner,),
    )
    (numer,) = call(
        numer_kernel,
        items,
        numbers_specs + [per_item(square), per_item(square)],
        [item_out(items, (NB, model_width), F32)],
        [],
        6 * tokens * NB * model_width,
        numbers + (hidden_high, hidden_low),
    )
    _, stats_whole, stats_after, numer = scan_over("seq", stats, seq_place, numer)

    numer = numer.reshape(items * NB, model_width)
    near, near_came = [], []
    down_exchange = Exchange(True)
    exchange_steps = down_exchange.steps
    for step, (axis, bit) in enumerate(down_exchange.orders[0]):
        if axis == "seq" and not down_exchange.shared(step):
            pairs = [(at, at ^ bit) for at in range(seq_count)]
            side = ((seq_place & bit) != 0).astype(jnp.int32)
            if near_came:
                numer = numer + near_came.pop().astype(F32)
            near.append((side, pairs))
            away, numer = halves(numer, side)
            away, stats_whole = lax.optimization_barrier((away.astype(BF16), stats_whole))
            near_came.append(lax.ppermute(away, "seq", pairs))
    back_specs = numbers_specs + [
        per_item(row), per_item(blocks), per_item((8, NB)), per_item((8, NB)),
        per_item((3 * STACK, model_width)),
    ]
    (
        down_sent, down_kept, up_sent, up_kept, d_attended, d_embed_direct, rows,
    ) = call(
        back_kernel,
        items,
        back_specs
        + [per_item(row), per_item(full), per_item(full)]
        + [per_item(square)] * 5
        + [whole((1, model_width)), whole((hidden_width, model_width)),
           whole((model_width, hidden_width)), whole((model_width, model_width))],
        halves_out(hidden_width, model_width)
        + halves_out(hidden_width + model_width, model_width, 16)
        + [
            item_out(items, square, BF16),
            total_out((vocab, model_width)),
            total_out((8, model_width)),
        ],
        [
            pltpu.VMEM((span, span), BF16),
            pltpu.VMEM((hidden_width, model_width), F32),
            pltpu.VMEM((hidden_width + model_width, model_width), F32),
        ],
        6 * tokens * hidden_width * model_width,
        numbers
        + (frontier, inner, stats_whole, stats_after, cot_stack, ids_own, act, slope,
           hidden_high, hidden_low, middle, normed_two, attended, norm2_gain[None],
           down_weight, up_weight, out_weight),
    )

    down = Chain(down_exchange, down_sent, down_kept)
    up = Chain(Exchange(False), up_sent, up_kept, rows)
    down.run(1)
    up.run(1)
    down.sent, up.sent, d_attended, near_came = lax.optimization_barrier(
        (down.sent, up.sent, d_attended, near_came)
    )
    down.rider = numer + near_came[0].astype(F32)
    down.start()
    up.start()
    rows_sent, rows_kept = call(
        attend_back_kernel,
        items,
        [scalars(), per_item((1, wide)), whole((vocab, 3 * model_width)),
         whole((model_width, vocab)), per_item(square), per_item((tiles * H // 2, 2 * TILE)),
         whole((vocab, model_width))],
        halves_out(4 * vocab, model_width),
        [
            pltpu.VMEM((4 * vocab, model_width), F32),
            pltpu.VMEM((3, SPAN_KEYS, 2 * TILE), F32),
            pltpu.VMEM((wide, 3 * model_width), BF16),
            pltpu.VMEM((model_width, wide), BF16),
            pltpu.VMEM((model_width, span), BF16),
            pltpu.VMEM((wide, model_width), F32),
            pltpu.VMEM((wide, model_width), F32),
            pltpu.VMEM((model_width, vocab), F32),
        ],
        10 * tokens * SPAN_KEYS * model_width,
        (place, ids_row, table, key_table, d_attended, logs, d_embed_direct),
    )

    rows_sent, down.came, up.came = lax.optimization_barrier((rows_sent, down.came, up.came))
    table_rows = Chain(Exchange(False), rows_sent, rows_kept, stop=exchange_steps - 2)
    chains = (up, down, table_rows)
    while any(chain.at < len(chain.plan) for chain in chains):
        ahead = None
        for chain in chains:
            if chain.at == len(chain.plan):
                continue
            if chain.came is None:
                chain.start()
            if ahead is not None:
                chain.came, _ = lax.optimization_barrier((chain.came, ahead))
            chain.finish()
            ahead = chain.sent if chain.cells is None else chain.cells
    d_rows = table_rows.cells
    d_weights = up.cells.astype(F32)
    d_down = down.cells.astype(F32)
    rows = up.vectors
    numer = down.rider
    for side, pairs in reversed(near):
        numer = joined(numer, lax.ppermute(numer, "seq", pairs), side)
    inverse = 1.0 / (stats_whole[:, 0] + 1.0)
    pooled = numer.astype(F32).reshape(items, NB, model_width) * inverse[:, :, None]
    d_up = jnp.concatenate(
        [
            d_weights[begin : begin + model_width]
            for begin in range(0, hidden_width, model_width)
        ],
        1,
    )
    d_out = d_weights[hidden_width:]
    d_embed, d_qkv, d_gain_one, d_shift_one = call(
        finish_kernel,
        1,
        [whole((vocab, model_width)), whole((vocab, model_width)), whole((1, model_width)),
         whole((model_width, 3 * model_width)), whole((4 * vocab, model_width))],
        [
            total_out((vocab, model_width)),
            total_out((model_width, 3 * model_width)),
            total_out((1, model_width)),
            total_out((1, model_width)),
        ],
        [],
        8 * vocab * model_width * model_width,
        (byte_embed, normed_one, norm1_gain[None], qkv_weight, d_rows),
    )
    return (
        pooled,
        d_embed,
        d_gain_one.reshape(-1),
        d_shift_one.reshape(-1),
        d_qkv,
        d_out,
        rows[0],
        rows[1],
        d_up,
        rows[4:].reshape(-1),
        d_down,
        rows[2],
        rows[3],
    )


def solution(mesh):
    placed = (P("dp", "seq"), P("dp"), P("dp")) + (P(),) * 12 + (P("dp", None, None),)
    return jax.shard_map(
        local,
        mesh=mesh,
        in_specs=placed,
        out_specs=(P("dp", None, None),) + (P(),) * 12,
        check_vma=False,
    )
```

```python
import functools

import jax
import jax.numpy as jnp
from jax import lax
from jax.experimental import pallas as pl
from jax.experimental.pallas import tpu as pltpu
from jax.sharding import PartitionSpec as P

H = 8
HD = 64
WIN = 64
NB = 64
TILE = 128
SPAN_KEYS = TILE + 2 * WIN
PAIR = 2 * HD
STACK = 80

eps = 1e-05
spread = 2.0
LOG2E = 1.4426950408889634
F32 = jnp.float32
BF16 = jnp.bfloat16
VMEM_BYTES = 56 * 1024 * 1024


def dot(left, right):
    return jnp.dot(left, right, preferred_element_type=F32)


def dot_last(left, right):
    return lax.dot_general(left, right, (((1,), (1,)), ((), ())), preferred_element_type=F32)


def dot_first(left, right):
    return lax.dot_general(left, right, (((0,), (0,)), ((), ())), preferred_element_type=F32)


def split_two_outside(value):
    high = lax.reduce_precision(value, 8, 7)
    return high.astype(BF16), (value - high).astype(BF16)


def split_two(value):
    high = value.astype(BF16)
    return high, (value - high.astype(F32)).astype(BF16)


def iota(shape, dim):
    return lax.broadcasted_iota(jnp.int32, shape, dim)


def one_hot_columns(ids_row, vocab):
    cells = iota((vocab, ids_row.shape[1]), 0)
    return jnp.where(cells == ids_row, 1.0, 0.0).astype(BF16)


def gelu_with_slope(value):
    below = 0.5 + 0.5 * lax.erf(value * 0.7071067811865476)
    bell = jnp.exp2(value * value * (-0.5 * LOG2E))
    return value * below, below + value * (bell * 0.3989422804014327)


def window_bias(first, last):
    key_at = iota((SPAN_KEYS, 2 * TILE), 0)
    query_at = iota((SPAN_KEYS, 2 * TILE), 1) & (TILE - 1)
    reach = key_at - query_at
    seen = (reach >= 0) & (reach <= 2 * WIN)
    seen_first = seen & (key_at >= WIN * first)
    seen_last = seen & (key_at < SPAN_KEYS - WIN * last)
    return [jnp.where(kept, 0.0, -1e30) for kept in (seen_first, seen, seen_last)]


def head_blocks(pair_rows):
    lane = iota(pair_rows.shape, 1)
    blank = jnp.zeros_like(pair_rows)
    return jnp.concatenate(
        [jnp.where(lane < HD, pair_rows, blank), jnp.where(lane < HD, blank, pair_rows)], 0
    )


def head_columns(pair_columns):
    return jnp.concatenate([pair_columns[:HD, :TILE], pair_columns[HD:, TILE:]], 0)


def running_sum(row, ones_matrix):
    one, rest = split_two(row)
    high = one.astype(F32) + rest.astype(F32)
    two = (row - high).astype(BF16)
    width = row.shape[1]
    parts = jnp.concatenate([one, rest, two, jnp.zeros((13, width), BF16)], 0)
    sums = dot(parts, ones_matrix)
    return sums[0:1] + sums[1:2] + sums[2:3]


def table_kernel(
    embed, gain, shift, weight,
    normed_out, table_out, key_out, value_out,
):
    rows = embed[...].astype(F32)
    centered = rows - jnp.mean(rows, -1, keepdims=True)
    scale = lax.rsqrt(jnp.mean(centered * centered, -1, keepdims=True) + eps)
    normed = (centered * scale * gain[...] + shift[...]).astype(BF16)
    normed_out[...] = normed
    model_width = rows.shape[1]
    table = dot(normed, weight[...])
    queries = table[:, :model_width].astype(BF16).astype(F32) * HD**-0.5
    table_out[:, :model_width] = queries.astype(BF16)
    table_out[:, model_width:] = table[:, model_width:].astype(BF16)
    key_out[...] = table[:, model_width : 2 * model_width].T.astype(BF16)
    value_out[...] = table[:, 2 * model_width :].T.astype(BF16)


def stacked_cot(cot, frontier_weight):
    rim = jnp.where(iota((STACK - NB, cot.shape[1]), 0) == 0, frontier_weight, 0.0)
    return split_two(jnp.concatenate([cot, rim], 0))


def take_turns(*parts):
    parts = list(parts)
    while parts:
        for part in list(parts):
            if next(part, None) is None:
                parts.remove(part)


def forward_kernel(
    place, lengths, ids_row, table, value_table, embed, out_weight, gain, shift,
    up_weight, up_bias, down_weight, down_bias, cot, frontier_weight,
    attended_out, log_out, middle_out, normed_out, act_out, slope_out, high_out, low_out,
    inner_out, frontier_out, running_out,
    bias, query_keys, value_columns, triangle, held_hot, held_attended,
):
    step = pl.program_id(0)
    items = pl.num_programs(0) - 1
    span = middle_out.shape[1]
    model_width = middle_out.shape[2]
    vocab = embed.shape[0]
    hidden_width = up_weight.shape[1]

    @pl.when(step == 0)
    def _():
        for at, tile in enumerate(window_bias(place[1], place[2])):
            bias[at] = tile
        triangle[...] = jnp.where(
            iota((span, span), 0) <= iota((span, span), 1), 1.0, 0.0
        ).astype(BF16)

    def attend():
        hot_columns = one_hot_columns(ids_row[0], vocab)
        hot = hot_columns.T
        query_keys[...] = dot(hot, table[:, : 2 * model_width]).astype(BF16)
        value_columns[...] = dot(value_table[...], hot_columns).astype(BF16)
        held_hot[...] = hot[WIN : WIN + span]
        yield True
        tiles = span // TILE
        pairs = H // 2
        for tile in range(tiles):
            begin = tile * TILE
            window = slice(begin, begin + SPAN_KEYS)
            tile_bias = bias[0 if tile == 0 else (2 if tile == tiles - 1 else 1)]
            lanes = [slice(pair * PAIR, (pair + 1) * PAIR) for pair in range(pairs)]
            scores = []
            for pair in range(pairs):
                key_lanes = slice(model_width + pair * PAIR, model_width + (pair + 1) * PAIR)
                query_block = head_blocks(query_keys[begin + WIN : begin + WIN + TILE, lanes[pair]])
                scores.append(dot_last(query_keys[window, key_lanes], query_block) + tile_bias)
            yield True
            probs = []
            for pair in range(pairs):
                peak = jnp.max(scores[pair], 0, keepdims=True)
                weights = jnp.exp(scores[pair] - peak)
                weight_sum = jnp.sum(weights, 0, keepdims=True)
                probs.append((weights * pltpu.reciprocal(weight_sum, approx=True)).astype(BF16))
                at = tile * pairs + pair
                log_out[0, at : at + 1, :] = peak + jnp.log(weight_sum)
            yield True
            mixed = [dot(value_columns[lanes[pair], window], probs[pair]) for pair in range(pairs)]
            for pair in range(pairs):
                rows = head_columns(mixed[pair]).T.astype(BF16)
                attended_out[0, begin : begin + TILE, lanes[pair]] = rows
                held_attended[begin : begin + TILE, lanes[pair]] = rows
            yield True

    def feed():
        middle = dot(held_hot[...], embed[...]) + dot(held_attended[...], out_weight[...])
        middle_out[0] = middle
        centered = middle - jnp.mean(middle, -1, keepdims=True)
        variance = jnp.mean(centered * centered, -1, keepdims=True)
        normed = (centered * lax.rsqrt(variance + eps) * gain[...] + shift[...]).astype(BF16)
        normed_out[0] = normed
        yield True
        chunk = 512
        cuts = [slice(begin, begin + chunk) for begin in range(0, hidden_width, chunk)]
        hidden = middle + down_bias[...]
        preact = dot(normed, up_weight[:, cuts[0]]) + up_bias[:, cuts[0]]
        for at, cells in enumerate(cuts):
            held = preact
            if at + 1 < len(cuts):
                preact = dot(normed, up_weight[:, cuts[at + 1]]) + up_bias[:, cuts[at + 1]]
            yield True
            act, slope = gelu_with_slope(held)
            act = act.astype(BF16)
            act_out[0, :, cells] = act
            slope_out[0, :, cells] = slope.astype(BF16)
            yield True
            hidden = hidden + dot(act, down_weight[cells, :])
            yield True
        high, low = split_two(hidden)
        high_out[0] = high
        low_out[0] = low
        cot_high, cot_low = stacked_cot(cot[0], frontier_weight[...])
        products = dot_last(jnp.concatenate([cot_high, cot_low], 0), high)
        inner = products[:STACK] + products[STACK:] + dot_last(cot_high, low)
        inner_out[0] = inner[:NB]
        frontier = 1.0 / (1.0 + jnp.exp(-inner[NB : NB + 1]))
        frontier_out[0] = frontier
        slot = place[0] + iota((1, span), 1)
        running_out[0] = running_sum(
            jnp.where(slot < lengths[step - 1], frontier, 0.0), triangle[...]
        )
        yield True

    @pl.when(step == 0)
    def _():
        take_turns(attend())

    @pl.when((step > 0) & (step < items))
    def _():
        take_turns(feed(), attend())

    @pl.when(step == items)
    def _():
        take_turns(feed())


def assignment(place, lengths, counts, before, total, running, item, held=0):
    span = running.shape[2]
    slot = place[0] + iota((1, span), 1)
    inside = slot < lengths[item]
    count = counts[item].astype(F32)
    position = count * (running[held] + before[item]) / total[item]
    block_at = iota((NB, span), 0)
    distance = position - (block_at.astype(F32) + 0.5)
    kept = inside & (block_at < counts[item])
    assign = jnp.where(kept, jnp.exp(-spread * distance * distance), 0.0)
    return position, assign, assign * distance * (-2.0 * spread), inside, count


def stats_kernel(place, lengths, counts, before, total, running, inner, stats_out):
    lane = iota((NB, 128), 1)
    for item in range(inner.shape[0]):
        position, assign, pull, _, _ = assignment(
            place, lengths, counts, before, total, running, item, item
        )
        products = inner[item]
        pull_inner = pull * products
        stats = jnp.zeros((NB, 128), F32)
        terms = (
            assign, assign * products, pull, pull_inner, pull * position, pull_inner * position,
        )
        for at, cells in enumerate(terms):
            stats = jnp.where(lane == at, jnp.sum(cells, 1, keepdims=True), stats)
        stats_out[item] = stats.T[:8]


def numer_kernel(place, lengths, counts, before, total, running, high, low, numer_out):
    _, assign, _, _, _ = assignment(
        place, lengths, counts, before, total, running, pl.program_id(0)
    )
    assign_high, assign_low = split_two(assign)
    numer_out[0] = (
        dot(assign_high, high[0]) + dot(assign_low, high[0]) + dot(assign_high, low[0])
    )


def hidden_gradient(
    place, lengths, counts, before, total, running, frontier, inner, whole_stats, after_stats,
    triangle,
):
    item = pl.program_id(0)
    span = running.shape[2]
    position, assign, pull, inside, count = assignment(
        place, lengths, counts, before, total, running, item
    )
    whole_columns = whole_stats[0].T
    after_columns = after_stats[0].T
    inverse = 1.0 / (whole_columns[:, 0:1] + 1.0)
    d_denom = -inverse * inverse * whole_columns[:, 1:2]
    push = jnp.sum(
        d_denom * after_columns[:, 2:3] + inverse * after_columns[:, 3:4], 0, keepdims=True
    )
    pushed = jnp.sum(
        d_denom * whole_columns[:, 4:5] + inverse * whole_columns[:, 5:6], 0, keepdims=True
    )
    d_position = jnp.sum((inner[0] * inverse + d_denom) * pull, 0, keepdims=True)
    d_cumulative = d_position * count / total[item]
    d_prob = running_sum(d_cumulative, triangle[...]) + (push * count - pushed) / total[item]
    share = frontier[0]
    d_logit = jnp.where(inside, d_prob * share * (1.0 - share), 0.0)
    left = jnp.concatenate(
        [assign * inverse, d_logit, jnp.zeros((STACK - NB - 1, span), F32)], 0
    )
    return split_two(left)


def write_halves(place, total, sent_out, kept_out):
    half = kept_out.shape[0]
    core = place[3]
    sent_out[:half] = total[pl.ds(pl.multiple_of((1 - core) * half, half), half)].astype(BF16)
    kept_out[...] = total[pl.ds(pl.multiple_of(core * half, half), half)].astype(BF16)


def suffix_ones(triangle):
    triangle[...] = jnp.where(
        iota(triangle.shape, 0) >= iota(triangle.shape, 1), 1.0, 0.0
    ).astype(BF16)


def back_kernel(
    place, lengths, counts, before, total, running, frontier, inner, whole_stats, after_stats,
    cot, frontier_weight, ids_row, act, slope, high, low, middle, normed, attended, gain, down_weight,
    up_weight, out_weight,
    down_sent, down_kept, up_sent, up_kept, attended_out, embed_out, rows_out,
    triangle, down_total, up_total,
):
    hidden_width = up_weight.shape[1]
    model_width = up_weight.shape[0]
    vocab = embed_out.shape[0]

    @pl.when(pl.program_id(0) == 0)
    def _():
        suffix_ones(triangle)
        for cells in (down_total, up_total, embed_out, rows_out):
            cells[...] = jnp.zeros_like(cells)

    left_high, left_low = hidden_gradient(
        place, lengths, counts, before, total, running, frontier, inner, whole_stats,
        after_stats, triangle,
    )
    cot_high, cot_low = stacked_cot(cot[0], frontier_weight[...])
    d_hidden = dot_first(
        jnp.concatenate([left_high, left_low, left_high], 0),
        jnp.concatenate([cot_high, cot_high, cot_low], 0),
    )
    d_low = d_hidden.astype(BF16)
    cuts = [
        slice(begin, begin + model_width) for begin in range(0, hidden_width, model_width)
    ]
    d_act = dot_last(d_low, down_weight[cuts[0], :])
    d_normed = None
    for at, cells in enumerate(cuts):
        held = d_act
        if at + 1 < len(cuts):
            d_act = dot_last(d_low, down_weight[cuts[at + 1], :])
        d_preact = (held * slope[0, :, cells].astype(F32)).astype(BF16)
        down_total[cells, :] += dot_first(act[0, :, cells], d_low)
        part = dot_last(d_preact, up_weight[:, cells])
        d_normed = part if d_normed is None else d_normed + part
        up_total[cells, :] += dot_first(normed[0], d_preact)
        rows_out[4 + at : 5 + at] += jnp.sum(d_preact.astype(F32), 0, keepdims=True)
    rows = middle[0]
    centered = rows - jnp.mean(rows, -1, keepdims=True)
    scale = lax.rsqrt(jnp.mean(centered * centered, -1, keepdims=True) + eps)
    unit = centered * scale
    tail = slice(NB, STACK)
    products = (
        dot(left_high[tail], high[0]) + dot(left_low[tail], high[0]) + dot(left_high[tail], low[0])
    )
    rows_out[2:3] += jnp.sum(d_low.astype(F32), 0, keepdims=True)
    rows_out[3:4] += products[0:1]
    rows_out[0:1] += jnp.sum(d_normed * unit, 0, keepdims=True)
    rows_out[1:2] += jnp.sum(d_normed, 0, keepdims=True)
    pushed = d_normed * gain[...]
    d_middle = d_hidden + scale * (
        pushed
        - jnp.mean(pushed, -1, keepdims=True)
        - unit * jnp.mean(pushed * unit, -1, keepdims=True)
    )
    middle_high, middle_low = split_two(d_middle)
    attended_out[0] = dot_last(middle_high, out_weight[...]).astype(BF16)
    up_total[hidden_width:, :] += dot_first(attended[0], middle_high)
    hot = one_hot_columns(ids_row[0], vocab)
    embed_out[...] += dot(hot, middle_high) + dot(hot, middle_low)

    @pl.when(pl.program_id(0) == pl.num_programs(0) - 1)
    def _():
        write_halves(place, down_total, down_sent, down_kept)
        write_halves(place, up_total, up_sent, up_kept)


def attend_back_kernel(
    place, ids_row, table, key_table, d_attended, logs, rows_in, vectors,
    *outs_and_scratch,
):
    *outs, rows_total, bias, table_rows, key_columns, d_queries, d_keys, d_values, (
        queries_total
    ) = outs_and_scratch
    item = pl.program_id(0)
    span = d_attended.shape[1]
    model_width = d_attended.shape[2]
    vocab = table.shape[0]

    @pl.when(item == 0)
    def _():
        for at, tile in enumerate(window_bias(place[1], place[2])):
            bias[at] = tile
        given = rows_in.shape[0]
        rows_total[:given] = rows_in[...]
        if given < 4 * vocab:
            rows_total[given:] = jnp.zeros((4 * vocab - given, model_width), F32)
        queries_total[...] = jnp.zeros_like(queries_total)

    hot_columns = one_hot_columns(ids_row[0], vocab)
    hot = hot_columns.T
    table_rows[...] = dot(hot, table[...]).astype(BF16)
    key_columns[...] = dot(key_table[...], hot_columns).astype(BF16)
    d_keys[...] = jnp.zeros_like(d_keys)
    d_values[...] = jnp.zeros_like(d_values)
    tiles = span // TILE
    pairs = H // 2
    for tile in range(tiles):
        begin = tile * TILE
        tile_bias = bias[0 if tile == 0 else (2 if tile == tiles - 1 else 1)]
        window = slice(begin, begin + SPAN_KEYS)
        lanes = [slice(pair * PAIR, (pair + 1) * PAIR) for pair in range(pairs)]
        query_blocks, grad_blocks, scores, d_probs = [], [], [], []
        for pair in range(pairs):
            key_lanes = slice(model_width + pair * PAIR, model_width + (pair + 1) * PAIR)
            value_lanes = slice(2 * model_width + pair * PAIR, 2 * model_width + (pair + 1) * PAIR)
            query_blocks.append(
                head_blocks(table_rows[begin + WIN : begin + WIN + TILE, lanes[pair]])
            )
            grad_blocks.append(head_blocks(d_attended[0, begin : begin + TILE, lanes[pair]]))
            scores.append(dot_last(table_rows[window, key_lanes], query_blocks[pair]) + tile_bias)
            d_probs.append(dot_last(table_rows[window, value_lanes], grad_blocks[pair]))
        probs_low, d_scores = [], []
        for pair in range(pairs):
            at = tile * pairs + pair
            probs = jnp.exp(scores[pair] - logs[0, at : at + 1, :])
            weighted = probs * d_probs[pair]
            probs_low.append(probs.astype(BF16))
            d_scores.append(
                (weighted - probs * jnp.sum(weighted, 0, keepdims=True)).astype(BF16)
            )
        for pair in range(pairs):
            d_values[window, lanes[pair]] += dot(probs_low[pair], grad_blocks[pair])
            d_keys[window, lanes[pair]] += dot(d_scores[pair], query_blocks[pair])
        turned = [dot(key_columns[lanes[pair], window], d_scores[pair]) for pair in range(pairs)]
        for pair in range(pairs):
            d_queries[lanes[pair], begin : begin + TILE] = (
                head_columns(turned[pair]) * (HD**-0.5)
            ).astype(BF16)
    queries_total[...] += dot(d_queries[...], hot[WIN : WIN + span])
    rows_total[2 * vocab : 3 * vocab] += dot(hot_columns, d_keys[...].astype(BF16))
    rows_total[3 * vocab :] += dot(hot_columns, d_values[...].astype(BF16))

    @pl.when(item == pl.num_programs(0) - 1)
    def _():
        rows_total[vocab : 2 * vocab] += queries_total[...].T
        write_halves(place, rows_total, *outs)
        vectors_high, vectors_low = split_two(vectors[...])
        outs[0][outs[1].shape[0] :] = jnp.concatenate([vectors_high, vectors_low], 0)


def finish_kernel(
    place, embed, normed, gain, weight, numer, stats, *refs,
):
    far = refs[:6]
    embed_out, gain_out, shift_out, pooled_out, down_out, up_out, out_out, weight_out = refs[6:14]
    near = refs[14:20]
    down_held, up_held, out_held, weight_held, arrived, left = refs[20:]
    vocab, model_width = embed.shape
    moves = [
        pltpu.make_async_copy(source, target, arrived.at[at])
        for at, (source, target) in enumerate(zip(far, near))
    ]
    sent = []

    def send(source, target):
        move = pltpu.make_async_copy(source, target, left.at[len(sent)])
        move.start()
        sent.append(move)

    def sides(at):
        moves[2 * at].wait()
        moves[2 * at + 1].wait()
        mine, came = near[2 * at][...], near[2 * at + 1][...]
        return [jnp.where(place[3] == core, mine, came) for core in (0, 1)]

    for move in moves:
        move.start()
    for core, side in enumerate(sides(0)):
        half = side.shape[0]
        for begin in range(0, half, half // 2):
            own = slice(core * half + begin, core * half + begin + half // 2)
            down_held[own] = side[begin : begin + half // 2].astype(F32)
            send(down_held.at[own], down_out.at[own])
    for core, side in enumerate(sides(1)):
        half = side.shape[0]
        step = model_width // 2
        for begin in range(0, half, step):
            lane, row = divmod(core * half + begin, model_width)
            cells = side[begin : begin + step].astype(F32)
            lanes = slice(lane * model_width, (lane + 1) * model_width)
            if lane * model_width < up_held.shape[1]:
                up_held[row : row + step, lanes] = cells
                if row:
                    send(up_held.at[:, lanes], up_out.at[:, lanes])
            else:
                out_held[row : row + step] = cells
                if row:
                    send(out_held, out_out)
    for item in range(stats.shape[0]):
        own = slice(item * NB, (item + 1) * NB)
        inverse = 1.0 / (stats[item].T[:, 0:1] + 1.0)
        pooled_out[item] = numer[own].astype(F32) * inverse
    sums = jnp.concatenate(sides(2), 0)
    rows = embed[...].astype(F32)
    centered = rows - jnp.mean(rows, -1, keepdims=True)
    scale = lax.rsqrt(jnp.mean(centered * centered, -1, keepdims=True) + eps)
    unit = centered * scale
    d_normed = None
    for at in range(3):
        lanes = slice(at * model_width, (at + 1) * model_width)
        part = sums[(at + 1) * vocab : (at + 2) * vocab]
        weight_held[:, lanes] = dot_first(normed[...], part)
        send(weight_held.at[:, lanes], weight_out.at[:, lanes])
        back = dot_last(part, weight[:, lanes])
        d_normed = back if d_normed is None else d_normed + back
    gain_out[...] = jnp.sum(d_normed * unit, 0, keepdims=True)
    shift_out[...] = jnp.sum(d_normed, 0, keepdims=True)
    pushed = d_normed * gain[...]
    embed_out[...] = sums[:vocab].astype(F32) + scale * (
        pushed
        - jnp.mean(pushed, -1, keepdims=True)
        - unit * jnp.mean(pushed * unit, -1, keepdims=True)
    )
    for move in sent:
        move.wait()


def whole(shape):
    return pl.BlockSpec(shape, lambda item: (0,) * len(shape))


def per_item(shape):
    return pl.BlockSpec((1,) + shape, lambda item: (item,) + (0,) * len(shape))


def item_from(shape, first):
    return pl.BlockSpec((1,) + shape, lambda item: (item + first,) + (0,) * len(shape))


def scalars():
    return pl.BlockSpec(memory_space=pltpu.SMEM)


def call(kernel, items, in_specs, outs, scratch, flops, arrays):
    flops = 1
    shapes = [jax.ShapeDtypeStruct(shape, dtype) for _, shape, dtype in outs]
    return pl.pallas_call(
        kernel,
        grid=(items,),
        in_specs=in_specs,
        out_specs=[spec for spec, _, _ in outs],
        out_shape=shapes,
        scratch_shapes=scratch,
        compiler_params=pltpu.CompilerParams(vmem_limit_bytes=VMEM_BYTES),
        cost_estimate=pl.CostEstimate(flops=flops, bytes_accessed=0, transcendentals=0),
    )(*arrays)


def item_out(items, shape, dtype):
    return per_item(shape), (items,) + shape, dtype


def halves_out(rows, width, more=0):
    return [total_out((rows // 2 + more, width), BF16), total_out((rows // 2, width), BF16)]


def total_out(shape, dtype=F32):
    return whole(shape), shape, dtype


def bits_of(count):
    return [1 << at for at in range(count.bit_length() - 1)]


def scan_over(axis, cells, index, beside=None):
    count = lax.axis_size(axis)
    earlier = jnp.zeros_like(cells)
    later = jnp.zeros_like(cells)
    for step, bit in enumerate(bits_of(count)):
        if step == 1 and beside is not None:
            cells, beside = lax.optimization_barrier((cells, beside))
        other = lax.ppermute(cells, axis, [(at, at ^ bit) for at in range(count)])
        upper = (index & bit) != 0
        earlier = earlier + jnp.where(upper, other, 0.0)
        later = later + jnp.where(upper, 0.0, other)
        cells = cells + other
    return earlier, cells, later, beside


def joined(mine, came, side):
    half = mine.shape[0]
    cells = jnp.zeros((2 * half,) + mine.shape[1:], mine.dtype)
    cells = lax.dynamic_update_slice_in_dim(cells, mine, side * half, 0)
    return lax.dynamic_update_slice_in_dim(cells, came, (1 - side) * half, 0)


class Exchange:
    def __init__(self, outer_first):
        outer_bits = [("dp", bit) for bit in bits_of(lax.axis_size("dp"))]
        inner_bits = [("seq", bit) for bit in bits_of(lax.axis_size("seq"))]
        core, last = outer_bits[:1], inner_bits[-1:]
        outer_bits, inner_bits = outer_bits[1:], inner_bits[:-1]
        if outer_first:
            cut = len(outer_bits)
            near, far = inner_bits[:cut], inner_bits[cut:]
            self.orders = (
                core + outer_bits + near + far + last,
                core + near + outer_bits + far + last,
            )
        else:
            self.orders = (
                core + inner_bits + outer_bits + last,
                core + inner_bits[::-1] + outer_bits + last,
            )
        self.steps = len(self.orders[0])

    def swap(self, cells, step):
        outer_size, inner_size = lax.axis_size("dp"), lax.axis_size("seq")
        pairs = []
        for flat in range(outer_size * inner_size):
            outer, inner = divmod(flat, inner_size)
            axis, bit = self.orders[outer & 1][step]
            other = (outer ^ bit, inner) if axis == "dp" else (outer, inner ^ bit)
            pairs.append((flat, other[0] * inner_size + other[1]))
        return lax.ppermute(cells, ("dp", "seq"), pairs)

    def side(self, step):
        sides = [
            ((lax.axis_index(axis) & bit) != 0).astype(jnp.int32)
            for axis, bit in (order[step] for order in self.orders)
        ]
        return jnp.where((lax.axis_index("dp") & 1) == 0, sides[0], sides[1])

    def shared(self, step):
        axis, _ = self.orders[0][step]
        return axis == "seq" and self.orders[0][step] == self.orders[1][step]


def halves(cells, side):
    half = cells.shape[0] // 2
    return (
        lax.dynamic_slice_in_dim(cells, (1 - side) * half, half, 0),
        lax.dynamic_slice_in_dim(cells, side * half, half, 0),
    )


class Chain:
    def __init__(self, exchange, sent, kept, vectors=None, stop=None):
        self.exchange = exchange
        self.sent = sent
        self.kept = kept
        self.cells = None
        self.vectors = vectors
        self.rider = None
        self.stop = exchange.steps if stop is None else stop
        gathers = range(self.stop - 1, -1, -1)
        self.plan = [("sum", step) for step in range(exchange.steps)]
        self.plan += [("gather", step) for step in gathers]
        self.at = 0
        self.came = None

    def start(self):
        kind, step = self.plan[self.at]
        if kind == "gather" or step >= self.stop:
            moved = [self.cells]
        else:
            moved = [self.sent]
        if self.vectors is not None and kind == "sum" and step > 0:
            moved += split_two_outside(self.vectors)
        if self.rider is not None and self.exchange.shared(step):
            if kind == "sum":
                away, self.rider = halves(self.rider, self.exchange.side(step))
                moved.append(away.astype(BF16))
            else:
                moved.append(self.rider.astype(BF16))
        moved = moved[0] if len(moved) == 1 else jnp.concatenate(moved, 0)
        self.came = self.exchange.swap(moved, step)

    def finish(self):
        kind, step = self.plan[self.at]
        came, self.came = self.came, None
        self.at += 1
        side = self.exchange.side(step)
        if kind == "gather":
            rows = self.cells.shape[0]
            if self.rider is not None and self.exchange.shared(step):
                self.rider = joined(self.rider.astype(BF16), came[rows:], side)
            if step == 0:
                self.last = came
            else:
                self.cells = joined(self.cells, came[:rows], side)
            return
        half = self.cells.shape[0] if step >= self.stop else self.kept.shape[0]
        if self.vectors is not None:
            rows = self.vectors.shape[0]
            high, low = split_two_outside(self.vectors)
            self.vectors = (high.astype(F32) + low.astype(F32)) + (
                came[half : half + rows].astype(F32)
                + came[half + rows : half + 2 * rows].astype(F32)
            )
        if step >= self.stop:
            self.cells = (self.cells.astype(F32) + came[:half].astype(F32)).astype(BF16)
            return
        if self.rider is not None and self.exchange.shared(step):
            self.rider = self.rider + came[half : half + self.rider.shape[0]].astype(F32)
        if step + 1 == self.stop:
            self.cells = (self.kept.astype(F32) + came[:half].astype(F32)).astype(BF16)
            return
        side = self.exchange.side(step + 1)
        away, stay = halves(self.kept, side)
        came_away, came_stay = halves(came[:half], side)
        self.sent = (away.astype(F32) + came_away.astype(F32)).astype(BF16)
        self.kept = stay.astype(F32) + came_stay.astype(F32)

    def run(self, until=None):
        until = len(self.plan) if until is None else until
        while self.at < until:
            if self.came is None:
                self.start()
            self.finish()


def local(
    byte_ids,
    item_lengths,
    block_counts,
    byte_embed,
    norm1_gain,
    norm1_shift,
    qkv_weight,
    out_weight,
    norm2_gain,
    norm2_shift,
    up_weight,
    up_bias,
    down_weight,
    down_bias,
    frontier_weight,
    pooled_cot,
):
    items, span = byte_ids.shape
    vocab, model_width = byte_embed.shape
    hidden_width = up_weight.shape[1]
    seq_count = lax.axis_size("seq")
    seq_place = lax.axis_index("seq")
    tokens = items * span
    wide = span + 2 * WIN
    tiles = span // TILE

    ends = range(seq_count - 1)
    ids_wide = jnp.concatenate(
        [
            lax.ppermute(byte_ids[:, span - WIN :], "seq", [(at, at + 1) for at in ends]),
            byte_ids,
            lax.ppermute(byte_ids[:, :WIN], "seq", [(at + 1, at) for at in ends]),
        ],
        1,
    )
    ids_row = ids_wide[:, None, :]
    ids_own = byte_ids[:, None, :]

    normed_one, table, key_table, value_table = call(
        table_kernel,
        1,
        [whole((vocab, model_width)), whole((1, model_width)), whole((1, model_width)),
         whole((model_width, 3 * model_width))],
        [
            total_out((vocab, model_width), BF16),
            total_out((vocab, 3 * model_width), BF16),
            total_out((model_width, vocab), BF16),
            total_out((model_width, vocab), BF16),
        ],
        [],
        6 * vocab * model_width * model_width,
        (byte_embed, norm1_gain[None], norm1_shift[None], qkv_weight),
    )

    first = (seq_place == 0).astype(jnp.int32)
    last = (seq_place == seq_count - 1).astype(jnp.int32)
    core = lax.axis_index("dp") & 1
    place = jnp.stack([seq_place * span, first, last, core]).astype(jnp.int32)

    square = (span, model_width)
    full = (span, hidden_width)
    row = (1, span)
    blocks = (NB, span)
    logs_shape = (tiles * H // 2, 2 * TILE)

    def item_ahead(shape):
        return pl.BlockSpec(
            (1,) + shape, lambda step: (jnp.minimum(step, items - 1),) + (0,) * len(shape)
        )

    def item_behind(shape):
        return pl.BlockSpec(
            (1,) + shape, lambda step: (jnp.maximum(step - 1, 0),) + (0,) * len(shape)
        )

    (
        attended, logs, middle, normed_two, act, slope, hidden_high, hidden_low,
        inner, frontier, running,
    ) = call(
        forward_kernel,
        items + 1,
        [scalars(), scalars(), item_ahead((1, wide))]
        + [
            whole(shape)
            for shape in (
                (vocab, 3 * model_width), (model_width, vocab), (vocab, model_width),
                (model_width, model_width), (1, model_width), (1, model_width),
                (model_width, hidden_width), (1, hidden_width),
                (hidden_width, model_width), (1, model_width),
            )
        ]
        + [item_behind((NB, model_width)), whole((1, model_width))],
        [
            (item_ahead(square), (items,) + square, BF16),
            (item_ahead(logs_shape), (items,) + logs_shape, F32),
        ]
        + [
            (item_behind(shape), (items,) + shape, dtype)
            for shape, dtype in (
                (square, F32), (square, BF16), (full, BF16), (full, BF16), (square, BF16),
                (square, BF16), (blocks, F32), (row, F32), (row, F32),
            )
        ],
        [
            pltpu.VMEM((3, SPAN_KEYS, 2 * TILE), F32),
            pltpu.VMEM((wide, 2 * model_width), BF16),
            pltpu.VMEM((model_width, wide), BF16),
            pltpu.VMEM((span, span), BF16),
            pltpu.VMEM((span, vocab), BF16),
            pltpu.VMEM(square, BF16),
        ],
        2 * tokens * model_width * (2 * hidden_width + 3 * model_width),
        (
            place, item_lengths, ids_row, table, value_table, byte_embed, out_weight,
            norm2_gain[None], norm2_shift[None], up_weight, up_bias[None], down_weight,
            down_bias[None], pooled_cot, frontier_weight[None],
        ),
    )

    mass_before, item_total, _, _ = scan_over("seq", running[:, 0, span - 1], seq_place)
    numbers = (place, item_lengths, block_counts, mass_before, item_total, running)
    numbers_specs = [scalars()] * 5 + [per_item(row)]

    (stats,) = call(
        stats_kernel,
        1,
        [scalars()] * 5 + [whole((items,) + row), whole((items,) + blocks)],
        [total_out((items, 8, NB))],
        [],
        tokens * NB,
        numbers + (inner,),
    )
    (numer,) = call(
        numer_kernel,
        items,
        numbers_specs + [per_item(square), per_item(square)],
        [item_out(items, (NB, model_width), F32)],
        [],
        6 * tokens * NB * model_width,
        numbers + (hidden_high, hidden_low),
    )
    _, stats_whole, stats_after, numer = scan_over("seq", stats, seq_place, numer)

    numer = numer.reshape(items * NB, model_width)
    near, near_came = [], []
    down_exchange = Exchange(True)
    exchange_steps = down_exchange.steps
    for step, (axis, bit) in enumerate(down_exchange.orders[0]):
        if axis == "seq" and not down_exchange.shared(step):
            pairs = [(at, at ^ bit) for at in range(seq_count)]
            side = ((seq_place & bit) != 0).astype(jnp.int32)
            if near_came:
                numer = numer + near_came.pop().astype(F32)
            near.append((side, pairs))
            away, numer = halves(numer, side)
            away, stats_whole = lax.optimization_barrier((away.astype(BF16), stats_whole))
            near_came.append(lax.ppermute(away, "seq", pairs))
    back_specs = numbers_specs + [
        per_item(row), per_item(blocks), per_item((8, NB)), per_item((8, NB)),
        per_item((NB, model_width)), whole((1, model_width)),
    ]
    (
        down_sent, down_kept, up_sent, up_kept, d_attended, d_embed_direct, rows,
    ) = call(
        back_kernel,
        items,
        back_specs
        + [per_item(row), per_item(full), per_item(full)]
        + [per_item(square)] * 5
        + [whole((1, model_width)), whole((hidden_width, model_width)),
           whole((model_width, hidden_width)), whole((model_width, model_width))],
        halves_out(hidden_width, model_width)
        + halves_out(hidden_width + model_width, model_width)
        + [
            item_out(items, square, BF16),
            total_out((vocab, model_width)),
            total_out((8, model_width)),
        ],
        [
            pltpu.VMEM((span, span), BF16),
            pltpu.VMEM((hidden_width, model_width), F32),
            pltpu.VMEM((hidden_width + model_width, model_width), F32),
        ],
        6 * tokens * hidden_width * model_width,
        numbers
        + (frontier, inner, stats_whole, stats_after, pooled_cot, frontier_weight[None], ids_own, act, slope,
           hidden_high, hidden_low, middle, normed_two, attended, norm2_gain[None],
           down_weight, up_weight, out_weight),
    )

    down = Chain(down_exchange, down_sent, down_kept)
    up = Chain(Exchange(False), up_sent, up_kept)
    down.run(1)
    up.run(1)
    down.sent, up.sent, d_attended, near_came = lax.optimization_barrier(
        (down.sent, up.sent, d_attended, near_came)
    )
    down.rider = numer + near_came[0].astype(F32)
    down.start()
    up.start()
    rows_sent, rows_kept = call(
        attend_back_kernel,
        items,
        [scalars(), per_item((1, wide)), whole((vocab, 3 * model_width)),
         whole((model_width, vocab)), per_item(square), per_item((tiles * H // 2, 2 * TILE)),
         whole((vocab, model_width)), whole((8, model_width))],
        halves_out(4 * vocab, model_width, 16),
        [
            pltpu.VMEM((4 * vocab, model_width), F32),
            pltpu.VMEM((3, SPAN_KEYS, 2 * TILE), F32),
            pltpu.VMEM((wide, 3 * model_width), BF16),
            pltpu.VMEM((model_width, wide), BF16),
            pltpu.VMEM((model_width, span), BF16),
            pltpu.VMEM((wide, model_width), F32),
            pltpu.VMEM((wide, model_width), F32),
            pltpu.VMEM((model_width, vocab), F32),
        ],
        10 * tokens * SPAN_KEYS * model_width,
        (place, ids_row, table, key_table, d_attended, logs, d_embed_direct, rows),
    )

    rows_sent, down.came, up.came = lax.optimization_barrier((rows_sent, down.came, up.came))
    table_rows = Chain(Exchange(False), rows_sent, rows_kept, rows, stop=exchange_steps - 2)
    numer = None
    ready = max(
        step for step in range(1, exchange_steps) if not down_exchange.shared(step)
    )
    turn = 0
    while any(chain.at < len(chain.plan) for chain in (up, down, table_rows)):
        chains = (table_rows, up, down) if turn < 1 else (up, down, table_rows)
        turn += 1
        ahead = None
        for chain in chains:
            if chain.at == len(chain.plan):
                continue
            if chain.came is None:
                chain.start()
            if ahead is not None:
                chain.came, _ = lax.optimization_barrier((chain.came, ahead))
            if numer is None and down.plan[down.at] == ("gather", ready):
                numer = down.rider
                for side, pairs in reversed(near[1:]):
                    numer = joined(numer, lax.ppermute(numer, "seq", pairs), side)
                numer_came = lax.ppermute(numer, "seq", near[0][1])
            if chain is table_rows and chain.plan[chain.at] == ("gather", 1):
                chain.came, numer_came = lax.optimization_barrier((chain.came, numer_came))
                numer = joined(numer, numer_came, near[0][0])
            chain.finish()
            ahead = chain.sent if chain.cells is None else chain.cells
    rows = table_rows.vectors
    arrived = [
        cells for chain in (down, up, table_rows) for cells in (chain.cells, chain.last)
    ]
    grads = (
        (hidden_width, model_width), (model_width, hidden_width), (model_width, model_width),
        (model_width, 3 * model_width),
    )
    anywhere = pl.BlockSpec(memory_space=pl.ANY)
    d_embed, d_gain_one, d_shift_one, pooled, d_down, d_up, d_out, d_qkv = call(
        finish_kernel,
        1,
        [scalars(), whole((vocab, model_width)), whole((vocab, model_width)),
         whole((1, model_width)), whole((model_width, 3 * model_width)),
         whole((items * NB, model_width)), whole((items, 8, NB))]
        + [anywhere] * 6,
        [
            total_out((vocab, model_width)),
            total_out((1, model_width)),
            total_out((1, model_width)),
            total_out((items, NB, model_width)),
        ]
        + [(anywhere, shape, F32) for shape in grads],
        [pltpu.VMEM(cells.shape, BF16) for cells in arrived]
        + [pltpu.VMEM(shape, F32) for shape in grads]
        + [pltpu.SemaphoreType.DMA((6,)), pltpu.SemaphoreType.DMA((12,))],
        8 * vocab * model_width * model_width,
        (place, byte_embed, normed_one, norm1_gain[None], qkv_weight, numer, stats_whole,
         *arrived),
    )
    return (
        pooled,
        d_embed,
        d_gain_one.reshape(-1),
        d_shift_one.reshape(-1),
        d_qkv,
        d_out,
        rows[0],
        rows[1],
        d_up,
        rows[4:].reshape(-1),
        d_down,
        rows[2],
        rows[3],
    )


def solution(mesh):
    placed = (P("dp", "seq"), P("dp"), P("dp")) + (P(),) * 12 + (P("dp", None, None),)
    return jax.shard_map(
        local,
        mesh=mesh,
        in_specs=placed,
        out_specs=(P("dp", None, None),) + (P(),) * 12,
        check_vma=False,
    )
```

```python
import functools

import jax
import jax.numpy as jnp
from jax import lax
from jax.experimental import pallas as pl
from jax.experimental.pallas import tpu as pltpu
from jax.sharding import PartitionSpec as P

H = 8
HD = 64
WIN = 64
NB = 64
TILE = 128
SPAN_KEYS = TILE + 2 * WIN
PAIR = 2 * HD
STACK = 80

eps = 1e-05
spread = 2.0
LOG2E = 1.4426950408889634
F32 = jnp.float32
BF16 = jnp.bfloat16
VMEM_BYTES = 56 * 1024 * 1024


def dot(left, right):
    return jnp.dot(left, right, preferred_element_type=F32)


def dot_last(left, right):
    return lax.dot_general(left, right, (((1,), (1,)), ((), ())), preferred_element_type=F32)


def dot_first(left, right):
    return lax.dot_general(left, right, (((0,), (0,)), ((), ())), preferred_element_type=F32)


def split_two_outside(value):
    high = lax.reduce_precision(value, 8, 7)
    return high.astype(BF16), (value - high).astype(BF16)


def split_two(value):
    high = value.astype(BF16)
    return high, (value - high.astype(F32)).astype(BF16)


def iota(shape, dim):
    return lax.broadcasted_iota(jnp.int32, shape, dim)


def one_hot_columns(ids_row, vocab):
    cells = iota((vocab, ids_row.shape[1]), 0)
    return jnp.where(cells == ids_row, 1.0, 0.0).astype(BF16)


def gelu_with_slope(value):
    below = 0.5 + 0.5 * lax.erf(value * 0.7071067811865476)
    bell = jnp.exp2(value * value * (-0.5 * LOG2E))
    return value * below, below + value * (bell * 0.3989422804014327)


def window_bias(first, last):
    key_at = iota((SPAN_KEYS, 2 * TILE), 0)
    query_at = iota((SPAN_KEYS, 2 * TILE), 1) & (TILE - 1)
    reach = key_at - query_at
    seen = (reach >= 0) & (reach <= 2 * WIN)
    seen_first = seen & (key_at >= WIN * first)
    seen_last = seen & (key_at < SPAN_KEYS - WIN * last)
    return [jnp.where(kept, 0.0, -1e30) for kept in (seen_first, seen, seen_last)]


def head_blocks(pair_rows):
    lane = iota(pair_rows.shape, 1)
    blank = jnp.zeros_like(pair_rows)
    return jnp.concatenate(
        [jnp.where(lane < HD, pair_rows, blank), jnp.where(lane < HD, blank, pair_rows)], 0
    )


def head_columns(pair_columns):
    return jnp.concatenate([pair_columns[:HD, :TILE], pair_columns[HD:, TILE:]], 0)


def running_sum(row, ones_matrix):
    one, rest = split_two(row)
    high = one.astype(F32) + rest.astype(F32)
    two = (row - high).astype(BF16)
    width = row.shape[1]
    parts = jnp.concatenate([one, rest, two, jnp.zeros((13, width), BF16)], 0)
    sums = dot(parts, ones_matrix)
    return sums[0:1] + sums[1:2] + sums[2:3]


def table_kernel(
    embed, gain, shift, weight,
    normed_out, table_out, key_out, value_out,
):
    rows = embed[...].astype(F32)
    centered = rows - jnp.mean(rows, -1, keepdims=True)
    scale = lax.rsqrt(jnp.mean(centered * centered, -1, keepdims=True) + eps)
    normed = (centered * scale * gain[...] + shift[...]).astype(BF16)
    normed_out[...] = normed
    model_width = rows.shape[1]
    table = dot(normed, weight[...])
    queries = table[:, :model_width].astype(BF16).astype(F32) * HD**-0.5
    table_out[:, :model_width] = queries.astype(BF16)
    table_out[:, model_width:] = table[:, model_width:].astype(BF16)
    key_out[...] = table[:, model_width : 2 * model_width].T.astype(BF16)
    value_out[...] = table[:, 2 * model_width :].T.astype(BF16)


def stacked_cot(cot, frontier_weight):
    rim = jnp.where(iota((STACK - NB, cot.shape[1]), 0) == 0, frontier_weight, 0.0)
    return split_two(jnp.concatenate([cot, rim], 0))


def take_turns(*parts):
    parts = list(parts)
    while parts:
        for part in list(parts):
            if next(part, None) is None:
                parts.remove(part)


def forward_kernel(
    place, lengths, ids_row, table, value_table, embed, out_weight, gain, shift,
    up_weight, up_bias, down_weight, down_bias, cot, frontier_weight,
    attended_out, log_out, middle_out, normed_out, act_out, slope_out, high_out, low_out,
    inner_out, frontier_out, running_out,
    bias, query_keys, value_columns, triangle, held_hot, held_attended,
):
    step = pl.program_id(0)
    items = pl.num_programs(0) - 1
    span = middle_out.shape[1]
    model_width = middle_out.shape[2]
    vocab = embed.shape[0]
    hidden_width = up_weight.shape[1]

    @pl.when(step == 0)
    def _():
        for at, tile in enumerate(window_bias(place[1], place[2])):
            bias[at] = tile
        triangle[...] = jnp.where(
            iota((span, span), 0) <= iota((span, span), 1), 1.0, 0.0
        ).astype(BF16)

    def attend():
        hot_columns = one_hot_columns(ids_row[0], vocab)
        hot = hot_columns.T
        query_keys[...] = dot(hot, table[:, : 2 * model_width]).astype(BF16)
        value_columns[...] = dot(value_table[...], hot_columns).astype(BF16)
        held_hot[...] = hot[WIN : WIN + span]
        yield True
        tiles = span // TILE
        pairs = H // 2
        for tile in range(tiles):
            begin = tile * TILE
            window = slice(begin, begin + SPAN_KEYS)
            tile_bias = bias[0 if tile == 0 else (2 if tile == tiles - 1 else 1)]
            lanes = [slice(pair * PAIR, (pair + 1) * PAIR) for pair in range(pairs)]
            scores = []
            for pair in range(pairs):
                key_lanes = slice(model_width + pair * PAIR, model_width + (pair + 1) * PAIR)
                query_block = head_blocks(query_keys[begin + WIN : begin + WIN + TILE, lanes[pair]])
                scores.append(dot_last(query_keys[window, key_lanes], query_block) + tile_bias)
            yield True
            probs = []
            for pair in range(pairs):
                peak = jnp.max(scores[pair], 0, keepdims=True)
                weights = jnp.exp(scores[pair] - peak)
                weight_sum = jnp.sum(weights, 0, keepdims=True)
                probs.append((weights * pltpu.reciprocal(weight_sum, approx=True)).astype(BF16))
                at = tile * pairs + pair
                log_out[0, at : at + 1, :] = peak + jnp.log(weight_sum)
            yield True
            mixed = [dot(value_columns[lanes[pair], window], probs[pair]) for pair in range(pairs)]
            for pair in range(pairs):
                rows = head_columns(mixed[pair]).T.astype(BF16)
                attended_out[0, begin : begin + TILE, lanes[pair]] = rows
                held_attended[begin : begin + TILE, lanes[pair]] = rows
            yield True

    def feed():
        middle = dot(held_hot[...], embed[...]) + dot(held_attended[...], out_weight[...])
        middle_out[0] = middle
        centered = middle - jnp.mean(middle, -1, keepdims=True)
        variance = jnp.mean(centered * centered, -1, keepdims=True)
        normed = (centered * lax.rsqrt(variance + eps) * gain[...] + shift[...]).astype(BF16)
        normed_out[0] = normed
        yield True
        chunk = 512
        cuts = [slice(begin, begin + chunk) for begin in range(0, hidden_width, chunk)]
        hidden = middle + down_bias[...]
        preact = dot(normed, up_weight[:, cuts[0]]) + up_bias[:, cuts[0]]
        for at, cells in enumerate(cuts):
            held = preact
            if at + 1 < len(cuts):
                preact = dot(normed, up_weight[:, cuts[at + 1]]) + up_bias[:, cuts[at + 1]]
            yield True
            act, slope = gelu_with_slope(held)
            act = act.astype(BF16)
            act_out[0, :, cells] = act
            slope_out[0, :, cells] = slope.astype(BF16)
            yield True
            hidden = hidden + dot(act, down_weight[cells, :])
            yield True
        high, low = split_two(hidden)
        high_out[0] = high
        low_out[0] = low
        cot_high, cot_low = stacked_cot(cot[0], frontier_weight[...])
        products = dot_last(jnp.concatenate([cot_high, cot_low], 0), high)
        inner = products[:STACK] + products[STACK:] + dot_last(cot_high, low)
        inner_out[0] = inner[:NB]
        frontier = 1.0 / (1.0 + jnp.exp(-inner[NB : NB + 1]))
        frontier_out[0] = frontier
        slot = place[0] + iota((1, span), 1)
        running_out[0] = running_sum(
            jnp.where(slot < lengths[step - 1], frontier, 0.0), triangle[...]
        )
        yield True

    @pl.when(step == 0)
    def _():
        take_turns(attend())

    @pl.when((step > 0) & (step < items))
    def _():
        take_turns(feed(), attend())

    @pl.when(step == items)
    def _():
        take_turns(feed())


def assignment(place, lengths, counts, before, total, running, item, held=0):
    span = running.shape[2]
    slot = place[0] + iota((1, span), 1)
    inside = slot < lengths[item]
    count = counts[item].astype(F32)
    position = count * (running[held] + before[item]) / total[item]
    block_at = iota((NB, span), 0)
    distance = position - (block_at.astype(F32) + 0.5)
    kept = inside & (block_at < counts[item])
    assign = jnp.where(kept, jnp.exp(-spread * distance * distance), 0.0)
    return position, assign, assign * distance * (-2.0 * spread), inside, count


def stats_kernel(place, lengths, counts, before, total, running, inner, stats_out):
    lane = iota((NB, 128), 1)
    for item in range(inner.shape[0]):
        position, assign, pull, _, _ = assignment(
            place, lengths, counts, before, total, running, item, item
        )
        products = inner[item]
        pull_inner = pull * products
        stats = jnp.zeros((NB, 128), F32)
        terms = (
            assign, assign * products, pull, pull_inner, pull * position, pull_inner * position,
        )
        for at, cells in enumerate(terms):
            stats = jnp.where(lane == at, jnp.sum(cells, 1, keepdims=True), stats)
        stats_out[item] = stats.T[:8]


def numer_kernel(place, lengths, counts, before, total, running, high, numer_out):
    _, assign, _, _, _ = assignment(
        place, lengths, counts, before, total, running, pl.program_id(0)
    )
    assign_high, assign_low = split_two(assign)
    numer_out[0] = dot(assign_high, high[0]) + dot(assign_low, high[0])


def hidden_gradient(
    place, lengths, counts, before, total, running, frontier, inner, whole_stats, after_stats,
    triangle,
):
    item = pl.program_id(0)
    span = running.shape[2]
    position, assign, pull, inside, count = assignment(
        place, lengths, counts, before, total, running, item
    )
    whole_columns = whole_stats[0].T
    after_columns = after_stats[0].T
    inverse = 1.0 / (whole_columns[:, 0:1] + 1.0)
    d_denom = -inverse * inverse * whole_columns[:, 1:2]
    push = jnp.sum(
        d_denom * after_columns[:, 2:3] + inverse * after_columns[:, 3:4], 0, keepdims=True
    )
    pushed = jnp.sum(
        d_denom * whole_columns[:, 4:5] + inverse * whole_columns[:, 5:6], 0, keepdims=True
    )
    d_position = jnp.sum((inner[0] * inverse + d_denom) * pull, 0, keepdims=True)
    d_cumulative = d_position * count / total[item]
    d_prob = running_sum(d_cumulative, triangle[...]) + (push * count - pushed) / total[item]
    share = frontier[0]
    d_logit = jnp.where(inside, d_prob * share * (1.0 - share), 0.0)
    left = jnp.concatenate(
        [assign * inverse, d_logit, jnp.zeros((STACK - NB - 1, span), F32)], 0
    )
    return split_two(left)


def write_halves(place, total, sent_out, kept_out):
    half = kept_out.shape[0]
    core = place[3]
    sent_out[:half] = total[pl.ds(pl.multiple_of((1 - core) * half, half), half)].astype(BF16)
    kept_out[...] = total[pl.ds(pl.multiple_of(core * half, half), half)].astype(BF16)


def suffix_ones(triangle):
    triangle[...] = jnp.where(
        iota(triangle.shape, 0) >= iota(triangle.shape, 1), 1.0, 0.0
    ).astype(BF16)


def back_kernel(
    place, lengths, counts, before, total, running, frontier, inner, whole_stats, after_stats,
    cot, frontier_weight, ids_row, act, slope, high, low, middle, normed, attended, gain, down_weight,
    up_weight, out_weight,
    down_sent, down_kept, up_sent, up_kept, attended_out, embed_out, rows_out,
    triangle, down_total, up_total,
):
    hidden_width = up_weight.shape[1]
    model_width = up_weight.shape[0]
    vocab = embed_out.shape[0]

    @pl.when(pl.program_id(0) == 0)
    def _():
        suffix_ones(triangle)
        for cells in (down_total, up_total, embed_out, rows_out):
            cells[...] = jnp.zeros_like(cells)

    left_high, left_low = hidden_gradient(
        place, lengths, counts, before, total, running, frontier, inner, whole_stats,
        after_stats, triangle,
    )
    cot_high, cot_low = stacked_cot(cot[0], frontier_weight[...])
    d_hidden = dot_first(
        jnp.concatenate([left_high, left_low, left_high], 0),
        jnp.concatenate([cot_high, cot_high, cot_low], 0),
    )
    d_low = d_hidden.astype(BF16)
    cuts = [
        slice(begin, begin + model_width) for begin in range(0, hidden_width, model_width)
    ]
    d_act = dot_last(d_low, down_weight[cuts[0], :])
    d_normed = None
    for at, cells in enumerate(cuts):
        held = d_act
        if at + 1 < len(cuts):
            d_act = dot_last(d_low, down_weight[cuts[at + 1], :])
        d_preact = (held * slope[0, :, cells].astype(F32)).astype(BF16)
        down_total[cells, :] += dot_first(act[0, :, cells], d_low)
        part = dot_last(d_preact, up_weight[:, cells])
        d_normed = part if d_normed is None else d_normed + part
        up_total[cells, :] += dot_first(normed[0], d_preact)
        rows_out[4 + at : 5 + at] += jnp.sum(d_preact.astype(F32), 0, keepdims=True)
    rows = middle[0]
    centered = rows - jnp.mean(rows, -1, keepdims=True)
    scale = lax.rsqrt(jnp.mean(centered * centered, -1, keepdims=True) + eps)
    unit = centered * scale
    tail = slice(NB, STACK)
    products = (
        dot(left_high[tail], high[0]) + dot(left_low[tail], high[0]) + dot(left_high[tail], low[0])
    )
    rows_out[2:3] += jnp.sum(d_low.astype(F32), 0, keepdims=True)
    rows_out[3:4] += products[0:1]
    rows_out[0:1] += jnp.sum(d_normed * unit, 0, keepdims=True)
    rows_out[1:2] += jnp.sum(d_normed, 0, keepdims=True)
    pushed = d_normed * gain[...]
    d_middle = d_hidden + scale * (
        pushed
        - jnp.mean(pushed, -1, keepdims=True)
        - unit * jnp.mean(pushed * unit, -1, keepdims=True)
    )
    middle_high, middle_low = split_two(d_middle)
    attended_out[0] = dot_last(middle_high, out_weight[...]).astype(BF16)
    up_total[hidden_width:, :] += dot_first(attended[0], middle_high)
    hot = one_hot_columns(ids_row[0], vocab)
    embed_out[...] += dot(hot, middle_high) + dot(hot, middle_low)

    @pl.when(pl.program_id(0) == pl.num_programs(0) - 1)
    def _():
        write_halves(place, down_total, down_sent, down_kept)
        write_halves(place, up_total, up_sent, up_kept)


def attend_back_kernel(
    place, ids_row, table, key_table, d_attended, logs, rows_in, vectors,
    *outs_and_scratch,
):
    *outs, rows_total, bias, table_rows, key_columns, d_queries, d_keys, d_values, (
        queries_total
    ) = outs_and_scratch
    item = pl.program_id(0)
    span = d_attended.shape[1]
    model_width = d_attended.shape[2]
    vocab = table.shape[0]

    @pl.when(item == 0)
    def _():
        for at, tile in enumerate(window_bias(place[1], place[2])):
            bias[at] = tile
        given = rows_in.shape[0]
        rows_total[:given] = rows_in[...]
        if given < 4 * vocab:
            rows_total[given:] = jnp.zeros((4 * vocab - given, model_width), F32)
        queries_total[...] = jnp.zeros_like(queries_total)

    hot_columns = one_hot_columns(ids_row[0], vocab)
    hot = hot_columns.T
    table_rows[...] = dot(hot, table[...]).astype(BF16)
    key_columns[...] = dot(key_table[...], hot_columns).astype(BF16)
    d_keys[...] = jnp.zeros_like(d_keys)
    d_values[...] = jnp.zeros_like(d_values)
    tiles = span // TILE
    pairs = H // 2
    for tile in range(tiles):
        begin = tile * TILE
        tile_bias = bias[0 if tile == 0 else (2 if tile == tiles - 1 else 1)]
        window = slice(begin, begin + SPAN_KEYS)
        lanes = [slice(pair * PAIR, (pair + 1) * PAIR) for pair in range(pairs)]
        query_blocks, grad_blocks, scores, d_probs = [], [], [], []
        for pair in range(pairs):
            key_lanes = slice(model_width + pair * PAIR, model_width + (pair + 1) * PAIR)
            value_lanes = slice(2 * model_width + pair * PAIR, 2 * model_width + (pair + 1) * PAIR)
            query_blocks.append(
                head_blocks(table_rows[begin + WIN : begin + WIN + TILE, lanes[pair]])
            )
            grad_blocks.append(head_blocks(d_attended[0, begin : begin + TILE, lanes[pair]]))
            scores.append(dot_last(table_rows[window, key_lanes], query_blocks[pair]) + tile_bias)
            d_probs.append(dot_last(table_rows[window, value_lanes], grad_blocks[pair]))
        probs_low, d_scores = [], []
        for pair in range(pairs):
            at = tile * pairs + pair
            probs = jnp.exp(scores[pair] - logs[0, at : at + 1, :])
            weighted = probs * d_probs[pair]
            probs_low.append(probs.astype(BF16))
            d_scores.append(
                (weighted - probs * jnp.sum(weighted, 0, keepdims=True)).astype(BF16)
            )
        for pair in range(pairs):
            d_values[window, lanes[pair]] += dot(probs_low[pair], grad_blocks[pair])
            d_keys[window, lanes[pair]] += dot(d_scores[pair], query_blocks[pair])
        turned = [dot(key_columns[lanes[pair], window], d_scores[pair]) for pair in range(pairs)]
        for pair in range(pairs):
            d_queries[lanes[pair], begin : begin + TILE] = (
                head_columns(turned[pair]) * (HD**-0.5)
            ).astype(BF16)
    queries_total[...] += dot(d_queries[...], hot[WIN : WIN + span])
    rows_total[2 * vocab : 3 * vocab] += dot(hot_columns, d_keys[...].astype(BF16))
    rows_total[3 * vocab :] += dot(hot_columns, d_values[...].astype(BF16))

    @pl.when(item == pl.num_programs(0) - 1)
    def _():
        rows_total[vocab : 2 * vocab] += queries_total[...].T
        write_halves(place, rows_total, *outs)
        vectors_high, vectors_low = split_two(vectors[...])
        outs[0][outs[1].shape[0] :] = jnp.concatenate([vectors_high, vectors_low], 0)


def finish_kernel(
    place, embed, normed, gain, weight, numer, stats, *refs,
):
    far = refs[:6]
    embed_out, gain_out, shift_out, pooled_out, down_out, up_out, out_out, weight_out = refs[6:14]
    near = refs[14:20]
    down_held, up_held, out_held, weight_held, arrived, left = refs[20:]
    vocab, model_width = embed.shape
    moves = [
        pltpu.make_async_copy(source, target, arrived.at[at])
        for at, (source, target) in enumerate(zip(far, near))
    ]
    sent = []

    def send(source, target):
        move = pltpu.make_async_copy(source, target, left.at[len(sent)])
        move.start()
        sent.append(move)

    def sides(at):
        moves[2 * at].wait()
        moves[2 * at + 1].wait()
        mine, came = near[2 * at][...], near[2 * at + 1][...]
        return [jnp.where(place[3] == core, mine, came) for core in (0, 1)]

    for move in moves:
        move.start()
    for core, side in enumerate(sides(0)):
        half = side.shape[0]
        for begin in range(0, half, half // 2):
            own = slice(core * half + begin, core * half + begin + half // 2)
            down_held[own] = side[begin : begin + half // 2].astype(F32)
            send(down_held.at[own], down_out.at[own])
    for core, side in enumerate(sides(1)):
        half = side.shape[0]
        step = model_width // 2
        for begin in range(0, half, step):
            lane, row = divmod(core * half + begin, model_width)
            cells = side[begin : begin + step].astype(F32)
            lanes = slice(lane * model_width, (lane + 1) * model_width)
            if lane * model_width < up_held.shape[1]:
                up_held[row : row + step, lanes] = cells
                if row:
                    send(up_held.at[:, lanes], up_out.at[:, lanes])
            else:
                out_held[row : row + step] = cells
                if row:
                    send(out_held, out_out)
    for item in range(stats.shape[0]):
        own = slice(item * NB, (item + 1) * NB)
        inverse = 1.0 / (stats[item].T[:, 0:1] + 1.0)
        pooled_out[item] = numer[own].astype(F32) * inverse
    sums = jnp.concatenate(sides(2), 0)
    rows = embed[...].astype(F32)
    centered = rows - jnp.mean(rows, -1, keepdims=True)
    scale = lax.rsqrt(jnp.mean(centered * centered, -1, keepdims=True) + eps)
    unit = centered * scale
    d_normed = None
    for at in range(3):
        lanes = slice(at * model_width, (at + 1) * model_width)
        part = sums[(at + 1) * vocab : (at + 2) * vocab]
        weight_held[:, lanes] = dot_first(normed[...], part)
        send(weight_held.at[:, lanes], weight_out.at[:, lanes])
        back = dot_last(part, weight[:, lanes])
        d_normed = back if d_normed is None else d_normed + back
    gain_out[...] = jnp.sum(d_normed * unit, 0, keepdims=True)
    shift_out[...] = jnp.sum(d_normed, 0, keepdims=True)
    pushed = d_normed * gain[...]
    embed_out[...] = sums[:vocab].astype(F32) + scale * (
        pushed
        - jnp.mean(pushed, -1, keepdims=True)
        - unit * jnp.mean(pushed * unit, -1, keepdims=True)
    )
    for move in sent:
        move.wait()


def whole(shape):
    return pl.BlockSpec(shape, lambda item: (0,) * len(shape))


def per_item(shape):
    return pl.BlockSpec((1,) + shape, lambda item: (item,) + (0,) * len(shape))


def item_from(shape, first):
    return pl.BlockSpec((1,) + shape, lambda item: (item + first,) + (0,) * len(shape))


def scalars():
    return pl.BlockSpec(memory_space=pltpu.SMEM)


def call(kernel, items, in_specs, outs, scratch, flops, arrays):
    flops = 1
    shapes = [jax.ShapeDtypeStruct(shape, dtype) for _, shape, dtype in outs]
    return pl.pallas_call(
        kernel,
        grid=(items,),
        in_specs=in_specs,
        out_specs=[spec for spec, _, _ in outs],
        out_shape=shapes,
        scratch_shapes=scratch,
        compiler_params=pltpu.CompilerParams(vmem_limit_bytes=VMEM_BYTES),
        cost_estimate=pl.CostEstimate(flops=flops, bytes_accessed=0, transcendentals=0),
    )(*arrays)


def item_out(items, shape, dtype):
    return per_item(shape), (items,) + shape, dtype


def halves_out(rows, width, more=0):
    return [total_out((rows // 2 + more, width), BF16), total_out((rows // 2, width), BF16)]


def total_out(shape, dtype=F32):
    return whole(shape), shape, dtype


def bits_of(count):
    return [1 << at for at in range(count.bit_length() - 1)]


def scan_over(axis, cells, index, beside=None):
    count = lax.axis_size(axis)
    earlier = jnp.zeros_like(cells)
    later = jnp.zeros_like(cells)
    for step, bit in enumerate(bits_of(count)):
        if step == 1 and beside is not None:
            cells, beside = lax.optimization_barrier((cells, beside))
        other = lax.ppermute(cells, axis, [(at, at ^ bit) for at in range(count)])
        upper = (index & bit) != 0
        earlier = earlier + jnp.where(upper, other, 0.0)
        later = later + jnp.where(upper, 0.0, other)
        cells = cells + other
    return earlier, cells, later, beside


def joined(mine, came, side):
    half = mine.shape[0]
    cells = jnp.zeros((2 * half,) + mine.shape[1:], mine.dtype)
    cells = lax.dynamic_update_slice_in_dim(cells, mine, side * half, 0)
    return lax.dynamic_update_slice_in_dim(cells, came, (1 - side) * half, 0)


class Exchange:
    def __init__(self, outer_first):
        outer_bits = [("dp", bit) for bit in bits_of(lax.axis_size("dp"))]
        inner_bits = [("seq", bit) for bit in bits_of(lax.axis_size("seq"))]
        core, last = outer_bits[:1], inner_bits[-1:]
        outer_bits, inner_bits = outer_bits[1:], inner_bits[:-1]
        if outer_first:
            cut = len(outer_bits)
            near, far = inner_bits[:cut], inner_bits[cut:]
            self.orders = (
                core + outer_bits + near + far + last,
                core + near + outer_bits + far + last,
            )
        else:
            self.orders = (
                core + inner_bits + outer_bits + last,
                core + inner_bits[::-1] + outer_bits + last,
            )
        self.steps = len(self.orders[0])

    def swap(self, cells, step):
        outer_size, inner_size = lax.axis_size("dp"), lax.axis_size("seq")
        pairs = []
        for flat in range(outer_size * inner_size):
            outer, inner = divmod(flat, inner_size)
            axis, bit = self.orders[outer & 1][step]
            other = (outer ^ bit, inner) if axis == "dp" else (outer, inner ^ bit)
            pairs.append((flat, other[0] * inner_size + other[1]))
        return lax.ppermute(cells, ("dp", "seq"), pairs)

    def side(self, step):
        sides = [
            ((lax.axis_index(axis) & bit) != 0).astype(jnp.int32)
            for axis, bit in (order[step] for order in self.orders)
        ]
        return jnp.where((lax.axis_index("dp") & 1) == 0, sides[0], sides[1])

    def shared(self, step):
        axis, _ = self.orders[0][step]
        return axis == "seq" and self.orders[0][step] == self.orders[1][step]


def halves(cells, side):
    half = cells.shape[0] // 2
    return (
        lax.dynamic_slice_in_dim(cells, (1 - side) * half, half, 0),
        lax.dynamic_slice_in_dim(cells, side * half, half, 0),
    )


class Chain:
    def __init__(self, exchange, sent, kept, vectors=None, stop=None):
        self.exchange = exchange
        self.sent = sent
        self.kept = kept
        self.cells = None
        self.vectors = vectors
        self.rider = None
        self.stop = exchange.steps if stop is None else stop
        gathers = range(self.stop - 1, -1, -1)
        self.plan = [("sum", step) for step in range(exchange.steps)]
        self.plan += [("gather", step) for step in gathers]
        self.at = 0
        self.came = None

    def start(self):
        kind, step = self.plan[self.at]
        if kind == "gather" or step >= self.stop:
            moved = [self.cells]
        else:
            moved = [self.sent]
        if self.vectors is not None and kind == "sum" and step > 0:
            moved += split_two_outside(self.vectors)
        if self.rider is not None and self.exchange.shared(step):
            if kind == "sum":
                away, self.rider = halves(self.rider, self.exchange.side(step))
                moved.append(away.astype(BF16))
            else:
                moved.append(self.rider.astype(BF16))
        moved = moved[0] if len(moved) == 1 else jnp.concatenate(moved, 0)
        self.came = self.exchange.swap(moved, step)

    def finish(self):
        kind, step = self.plan[self.at]
        came, self.came = self.came, None
        self.at += 1
        side = self.exchange.side(step)
        if kind == "gather":
            rows = self.cells.shape[0]
            if self.rider is not None and self.exchange.shared(step):
                self.rider = joined(self.rider.astype(BF16), came[rows:], side)
            if step == 0:
                self.last = came
            else:
                self.cells = joined(self.cells, came[:rows], side)
            return
        half = self.cells.shape[0] if step >= self.stop else self.kept.shape[0]
        if self.vectors is not None:
            rows = self.vectors.shape[0]
            high, low = split_two_outside(self.vectors)
            self.vectors = (high.astype(F32) + low.astype(F32)) + (
                came[half : half + rows].astype(F32)
                + came[half + rows : half + 2 * rows].astype(F32)
            )
        if step >= self.stop:
            self.cells = (self.cells.astype(F32) + came[:half].astype(F32)).astype(BF16)
            return
        if self.rider is not None and self.exchange.shared(step):
            self.rider = self.rider + came[half : half + self.rider.shape[0]].astype(F32)
        if step + 1 == self.stop:
            self.cells = (self.kept.astype(F32) + came[:half].astype(F32)).astype(BF16)
            return
        side = self.exchange.side(step + 1)
        away, stay = halves(self.kept, side)
        came_away, came_stay = halves(came[:half], side)
        self.sent = (away.astype(F32) + came_away.astype(F32)).astype(BF16)
        self.kept = stay.astype(F32) + came_stay.astype(F32)

    def run(self, until=None):
        until = len(self.plan) if until is None else until
        while self.at < until:
            if self.came is None:
                self.start()
            self.finish()


def local(
    byte_ids,
    item_lengths,
    block_counts,
    byte_embed,
    norm1_gain,
    norm1_shift,
    qkv_weight,
    out_weight,
    norm2_gain,
    norm2_shift,
    up_weight,
    up_bias,
    down_weight,
    down_bias,
    frontier_weight,
    pooled_cot,
):
    items, span = byte_ids.shape
    vocab, model_width = byte_embed.shape
    hidden_width = up_weight.shape[1]
    seq_count = lax.axis_size("seq")
    seq_place = lax.axis_index("seq")
    tokens = items * span
    wide = span + 2 * WIN
    tiles = span // TILE

    ends = range(seq_count - 1)
    ids_wide = jnp.concatenate(
        [
            lax.ppermute(byte_ids[:, span - WIN :], "seq", [(at, at + 1) for at in ends]),
            byte_ids,
            lax.ppermute(byte_ids[:, :WIN], "seq", [(at + 1, at) for at in ends]),
        ],
        1,
    )
    ids_row = ids_wide[:, None, :]
    ids_own = byte_ids[:, None, :]

    normed_one, table, key_table, value_table = call(
        table_kernel,
        1,
        [whole((vocab, model_width)), whole((1, model_width)), whole((1, model_width)),
         whole((model_width, 3 * model_width))],
        [
            total_out((vocab, model_width), BF16),
            total_out((vocab, 3 * model_width), BF16),
            total_out((model_width, vocab), BF16),
            total_out((model_width, vocab), BF16),
        ],
        [],
        6 * vocab * model_width * model_width,
        (byte_embed, norm1_gain[None], norm1_shift[None], qkv_weight),
    )

    first = (seq_place == 0).astype(jnp.int32)
    last = (seq_place == seq_count - 1).astype(jnp.int32)
    core = lax.axis_index("dp") & 1
    place = jnp.stack([seq_place * span, first, last, core]).astype(jnp.int32)

    square = (span, model_width)
    full = (span, hidden_width)
    row = (1, span)
    blocks = (NB, span)
    logs_shape = (tiles * H // 2, 2 * TILE)

    def item_ahead(shape):
        return pl.BlockSpec(
            (1,) + shape, lambda step: (jnp.minimum(step, items - 1),) + (0,) * len(shape)
        )

    def item_behind(shape):
        return pl.BlockSpec(
            (1,) + shape, lambda step: (jnp.maximum(step - 1, 0),) + (0,) * len(shape)
        )

    (
        attended, logs, middle, normed_two, act, slope, hidden_high, hidden_low,
        inner, frontier, running,
    ) = call(
        forward_kernel,
        items + 1,
        [scalars(), scalars(), item_ahead((1, wide))]
        + [
            whole(shape)
            for shape in (
                (vocab, 3 * model_width), (model_width, vocab), (vocab, model_width),
                (model_width, model_width), (1, model_width), (1, model_width),
                (model_width, hidden_width), (1, hidden_width),
                (hidden_width, model_width), (1, model_width),
            )
        ]
        + [item_behind((NB, model_width)), whole((1, model_width))],
        [
            (item_ahead(square), (items,) + square, BF16),
            (item_ahead(logs_shape), (items,) + logs_shape, F32),
        ]
        + [
            (item_behind(shape), (items,) + shape, dtype)
            for shape, dtype in (
                (square, F32), (square, BF16), (full, BF16), (full, BF16), (square, BF16),
                (square, BF16), (blocks, F32), (row, F32), (row, F32),
            )
        ],
        [
            pltpu.VMEM((3, SPAN_KEYS, 2 * TILE), F32),
            pltpu.VMEM((wide, 2 * model_width), BF16),
            pltpu.VMEM((model_width, wide), BF16),
            pltpu.VMEM((span, span), BF16),
            pltpu.VMEM((span, vocab), BF16),
            pltpu.VMEM(square, BF16),
        ],
        2 * tokens * model_width * (2 * hidden_width + 3 * model_width),
        (
            place, item_lengths, ids_row, table, value_table, byte_embed, out_weight,
            norm2_gain[None], norm2_shift[None], up_weight, up_bias[None], down_weight,
            down_bias[None], pooled_cot, frontier_weight[None],
        ),
    )

    mass_before, item_total, _, _ = scan_over("seq", running[:, 0, span - 1], seq_place)
    numbers = (place, item_lengths, block_counts, mass_before, item_total, running)
    numbers_specs = [scalars()] * 5 + [per_item(row)]

    (stats,) = call(
        stats_kernel,
        1,
        [scalars()] * 5 + [whole((items,) + row), whole((items,) + blocks)],
        [total_out((items, 8, NB))],
        [],
        tokens * NB,
        numbers + (inner,),
    )
    (numer,) = call(
        numer_kernel,
        items,
        numbers_specs + [per_item(square)],
        [item_out(items, (NB, model_width), F32)],
        [],
        6 * tokens * NB * model_width,
        numbers + (hidden_high,),
    )
    _, stats_whole, stats_after, numer = scan_over("seq", stats, seq_place, numer)

    numer = numer.reshape(items * NB, model_width)
    near, near_came = [], []
    down_exchange = Exchange(True)
    exchange_steps = down_exchange.steps
    for step, (axis, bit) in enumerate(down_exchange.orders[0]):
        if axis == "seq" and not down_exchange.shared(step):
            pairs = [(at, at ^ bit) for at in range(seq_count)]
            side = ((seq_place & bit) != 0).astype(jnp.int32)
            if near_came:
                numer = numer + near_came.pop().astype(F32)
            near.append((side, pairs))
            away, numer = halves(numer, side)
            away, stats_whole = lax.optimization_barrier((away.astype(BF16), stats_whole))
            near_came.append(lax.ppermute(away, "seq", pairs))
    back_specs = numbers_specs + [
        per_item(row), per_item(blocks), per_item((8, NB)), per_item((8, NB)),
        per_item((NB, model_width)), whole((1, model_width)),
    ]
    (
        down_sent, down_kept, up_sent, up_kept, d_attended, d_embed_direct, rows,
    ) = call(
        back_kernel,
        items,
        back_specs
        + [per_item(row), per_item(full), per_item(full)]
        + [per_item(square)] * 5
        + [whole((1, model_width)), whole((hidden_width, model_width)),
           whole((model_width, hidden_width)), whole((model_width, model_width))],
        halves_out(hidden_width, model_width)
        + halves_out(hidden_width + model_width, model_width)
        + [
            item_out(items, square, BF16),
            total_out((vocab, model_width)),
            total_out((8, model_width)),
        ],
        [
            pltpu.VMEM((span, span), BF16),
            pltpu.VMEM((hidden_width, model_width), F32),
            pltpu.VMEM((hidden_width + model_width, model_width), F32),
        ],
        6 * tokens * hidden_width * model_width,
        numbers
        + (frontier, inner, stats_whole, stats_after, pooled_cot, frontier_weight[None], ids_own, act, slope,
           hidden_high, hidden_low, middle, normed_two, attended, norm2_gain[None],
           down_weight, up_weight, out_weight),
    )

    down = Chain(down_exchange, down_sent, down_kept)
    up = Chain(Exchange(False), up_sent, up_kept)
    down.run(1)
    up.run(1)
    down.sent, up.sent, d_attended, near_came = lax.optimization_barrier(
        (down.sent, up.sent, d_attended, near_came)
    )
    down.rider = numer + near_came[0].astype(F32)
    down.start()
    up.start()
    rows_sent, rows_kept = call(
        attend_back_kernel,
        items,
        [scalars(), per_item((1, wide)), whole((vocab, 3 * model_width)),
         whole((model_width, vocab)), per_item(square), per_item((tiles * H // 2, 2 * TILE)),
         whole((vocab, model_width)), whole((8, model_width))],
        halves_out(4 * vocab, model_width, 16),
        [
            pltpu.VMEM((4 * vocab, model_width), F32),
            pltpu.VMEM((3, SPAN_KEYS, 2 * TILE), F32),
            pltpu.VMEM((wide, 3 * model_width), BF16),
            pltpu.VMEM((model_width, wide), BF16),
            pltpu.VMEM((model_width, span), BF16),
            pltpu.VMEM((wide, model_width), F32),
            pltpu.VMEM((wide, model_width), F32),
            pltpu.VMEM((model_width, vocab), F32),
        ],
        10 * tokens * SPAN_KEYS * model_width,
        (place, ids_row, table, key_table, d_attended, logs, d_embed_direct, rows),
    )

    rows_sent, down.came, up.came = lax.optimization_barrier((rows_sent, down.came, up.came))
    table_rows = Chain(Exchange(False), rows_sent, rows_kept, rows, stop=exchange_steps - 2)
    numer = None
    ready = max(
        step for step in range(1, exchange_steps) if not down_exchange.shared(step)
    )
    turn = 0
    while any(chain.at < len(chain.plan) for chain in (up, down, table_rows)):
        chains = (table_rows, up, down) if turn < 1 else (up, down, table_rows)
        turn += 1
        ahead = None
        for chain in chains:
            if chain.at == len(chain.plan):
                continue
            if chain.came is None:
                chain.start()
            if ahead is not None:
                chain.came, _ = lax.optimization_barrier((chain.came, ahead))
            if numer is None and down.plan[down.at] == ("gather", ready):
                numer = down.rider
                for side, pairs in reversed(near[1:]):
                    numer = joined(numer, lax.ppermute(numer, "seq", pairs), side)
                numer_came = lax.ppermute(numer, "seq", near[0][1])
            if chain is table_rows and chain.plan[chain.at] == ("gather", 1):
                chain.came, numer_came = lax.optimization_barrier((chain.came, numer_came))
                numer = joined(numer, numer_came, near[0][0])
            chain.finish()
            ahead = chain.sent if chain.cells is None else chain.cells
    rows = table_rows.vectors
    arrived = [
        cells for chain in (down, up, table_rows) for cells in (chain.cells, chain.last)
    ]
    grads = (
        (hidden_width, model_width), (model_width, hidden_width), (model_width, model_width),
        (model_width, 3 * model_width),
    )
    anywhere = pl.BlockSpec(memory_space=pl.ANY)
    d_embed, d_gain_one, d_shift_one, pooled, d_down, d_up, d_out, d_qkv = call(
        finish_kernel,
        1,
        [scalars(), whole((vocab, model_width)), whole((vocab, model_width)),
         whole((1, model_width)), whole((model_width, 3 * model_width)),
         whole((items * NB, model_width)), whole((items, 8, NB))]
        + [anywhere] * 6,
        [
            total_out((vocab, model_width)),
            total_out((1, model_width)),
            total_out((1, model_width)),
            total_out((items, NB, model_width)),
        ]
        + [(anywhere, shape, F32) for shape in grads],
        [pltpu.VMEM(cells.shape, BF16) for cells in arrived]
        + [pltpu.VMEM(shape, F32) for shape in grads]
        + [pltpu.SemaphoreType.DMA((6,)), pltpu.SemaphoreType.DMA((12,))],
        8 * vocab * model_width * model_width,
        (place, byte_embed, normed_one, norm1_gain[None], qkv_weight, numer, stats_whole,
         *arrived),
    )
    return (
        pooled,
        d_embed,
        d_gain_one.reshape(-1),
        d_shift_one.reshape(-1),
        d_qkv,
        d_out,
        rows[0],
        rows[1],
        d_up,
        rows[4:].reshape(-1),
        d_down,
        rows[2],
        rows[3],
    )


def solution(mesh):
    placed = (P("dp", "seq"), P("dp"), P("dp")) + (P(),) * 12 + (P("dp", None, None),)
    return jax.shard_map(
        local,
        mesh=mesh,
        in_specs=placed,
        out_specs=(P("dp", None, None),) + (P(),) * 12,
        check_vma=False,
    )
```
